32 devices in a mesh: ctx: 16 (over z, y, core), tp: 2 (over x).
Axes of the slice: x: 2, y: 2, z: 4, core: 2. Of those that a mesh axis runs over, the one named last changes fastest.
Arguments:
- cache_k: bfloat16 [4096, 1024], P('ctx', 'tp'), may hold values from -8 to 8
- cache_v: bfloat16 [4096, 1024], P('ctx', 'tp'), may hold values from -6 to 6
- span_q: bfloat16 [64, 4096], P('ctx', 'tp'), may hold values from -8 to 8
- span_k: bfloat16 [64, 1024], P('ctx', 'tp'), may hold values from -6 to 6
- span_v: bfloat16 [64, 1024], P('ctx', 'tp'), may hold values from -6 to 6
- span_frames: int32 [64], replicated, may hold values from 0 to 7, never falling along the last dimension, each value on 1 to 16 neighbouring positions
- action_ids: int32 [64], P('ctx'), may hold values from 0 to 17
- action_table: bfloat16 [18, 1024], P(None, 'tp'), may hold values from -6 to 6
- frame_q: bfloat16 [64, 4096], P('ctx', 'tp'), may hold values from -8 to 8
- frame_k: bfloat16 [64, 1024], P('ctx', 'tp'), may hold values from -6 to 6
- frame_v: bfloat16 [64, 1024], P('ctx', 'tp'), may hold values from -6 to 6
- revealed_k: bfloat16 [64, 1024], P('ctx', 'tp'), may hold values from -6 to 6
- revealed_v: bfloat16 [64, 1024], P('ctx', 'tp'), may hold values from -6 to 6
- mask_k: bfloat16 [1024], P('tp'), may hold values from -6 to 6
- mask_v: bfloat16 [1024], P('tp'), may hold values from -6 to 6
- pass1_idx: int32 [32], replicated, may hold values from 0 to 63, as said below
- pass2_idx: int32 [16], replicated, may hold values from 0 to 63, as said below
- out_gain: float32 [4096], P('tp'), may hold values from 0.5 to 1.5
Outputs:
- span_out: bfloat16 [64, 4096], P('ctx', 'tp')
- first_out: bfloat16 [32, 4096], P('ctx', 'tp')
- second_out: bfloat16 [16, 4096], P('ctx', 'tp')
The draws below stay inside these ranges and needn't reach their ends.
Inputs may be any that keep to these rules, and one draw needn't show every extreme that they name: `pass1_idx`: 32 distinct frame positions, 0 and 63 among them. `pass2_idx`: 16 distinct entries of pass1_idx, 0 and 63 among them.
All inputs are finite; a program needn't handle non-finite values.
Results may differ from the reference program's by a relative error of at most 0.0095.
Values may be sent and summed in bfloat16 or wider, within the bound.
No kernel may reach another device: no remote copies, remote signals or barrier semaphores. Data moves between devices by JAX's collectives and lax.ppermute only.
A program may use at most 64 MiB of HBM per device.

```python
import math
import jax
import jax.numpy as jnp
import numpy as np
from jax import lax

H = 32
KVH = 8
HD = 128
ACTIONS = 18
CACHE = 4096
SPAN = 64
FRAME = 64
MASK1 = 32
MASK2 = 16


def masked_base(key):
    middle = jax.random.permutation(jax.random.fold_in(key, 5), FRAME - 2).astype(jnp.int32) + 1
    return jnp.concatenate([jnp.array([0, FRAME - 1], jnp.int32), middle[:MASK1 - 2]])


def draw_cache_k(key, part):
    backdrop = jnp.clip(jax.random.normal(jax.random.fold_in(key, 1), (CACHE, KVH * HD), jnp.float32), -6.0, 6.0)
    return backdrop.astype(jnp.bfloat16)


def draw_span_q(key, part):
    backdrop = jnp.clip(jax.random.normal(jax.random.fold_in(key, 2), (SPAN, H * HD), jnp.float32), -6.0, 6.0)
    return backdrop.astype(jnp.bfloat16)


def draw_frame_q(key, part):
    backdrop = jnp.clip(jax.random.normal(jax.random.fold_in(key, 3), (FRAME, H * HD), jnp.float32), -6.0, 6.0)
    return backdrop.astype(jnp.bfloat16)


def draw_pass1_idx(key, part):
    base_rows = masked_base(key)
    order = jax.random.permutation(jax.random.fold_in(key, 6), MASK1)
    return base_rows[order].astype(jnp.int32)


def draw_pass2_idx(key, part):
    base_rows = masked_base(key)[:MASK2]
    order = jax.random.permutation(jax.random.fold_in(key, 7), MASK2)
    return base_rows[order].astype(jnp.int32)


def place_ends(drawn, own_key, low, high):
    extent = drawn.shape
    index_at = [jax.random.randint(jax.random.fold_in(own_key, axis), (), 0, extent[axis]) for axis in range(len(extent))]
    drawn = drawn.at[tuple(index_at)].set(low)
    longest = extent.index(max(extent))
    index_at[longest] = (index_at[longest] + 1) % extent[longest]
    return drawn.at[tuple(index_at)].set(high)


def levels(rng, dims, shards, least, top_value):
    factor_of = 1.0
    for position, shards_of in shards:
        draws = jax.random.uniform(jax.random.fold_in(jax.random.fold_in(rng, 6), position), (shards_of,), jnp.float32, least / len(shards), top_value / len(shards))
        factor_of = factor_of * jnp.repeat(jnp.exp(draws), dims[position] // shards_of).reshape((-1,) + (1,) * (len(dims) - 1 - position))
    return factor_of


def length_profile(number_of, total, bound, lean):
    loads = [(1 << 20) // math.isqrt(rank ** lean) + 1 for rank in range(2, number_of + 1)]
    surplus, given = total - bound - (number_of - 1), [1] * (number_of - 1)
    while surplus > 0:
        movable = [i for i in range(number_of - 1) if given[i] < bound]
        whole, remaining = sum([loads[i] for i in movable]), surplus
        for i in movable:
            extra = min(bound - given[i], max(1, remaining * loads[i] // whole), surplus)
            given[i] = given[i] + extra
            surplus = surplus - extra
    return np.array([bound] + given)


def uneven_parts(own_key, count, total, bound, slope):
    if count == 2:
        one = jax.random.randint(own_key, (), max(1, total - bound), min(bound, total - 1) + 1)
        return jnp.stack([one, total - one])
    tallies = jnp.asarray(length_profile(count, total, bound, slope), jnp.int32)
    couples = (count - 1) // 2
    source_of, taker = tallies[1:1 + 2 * couples:2], tallies[2:2 + 2 * couples:2]
    slack = jnp.minimum(source_of - 1, bound - taker)
    moved = jax.random.randint(jax.random.fold_in(own_key, 1), (couples,), 0, 1 << 20) % (slack + 1)
    tallies = tallies.at[1:1 + 2 * couples:2].set(source_of - moved).at[2:2 + 2 * couples:2].set(taker + moved)
    return tallies[jax.random.permutation(jax.random.fold_in(own_key, 2), count)]


def bell_draw(own_key, dims, scale, bound, pieces=(), held_as=jnp.bfloat16):
    values = jax.random.normal(own_key, dims, jnp.float32) * scale
    if len(pieces) > 0:
        values = levels(own_key, dims, pieces, -0.22, 0.18) * values
    return jnp.clip(values, min=-bound, max=bound).astype(held_as)


def setup_inputs(seed: int = 0) -> dict:
    seeds = jax.random.split(jax.random.key(seed), 19)
    return {
        "cache_k": draw_cache_k(jax.random.fold_in(seeds[18], 71), 0),
        "cache_v": bell_draw(seeds[1], (CACHE, KVH * HD), 1.0, 6.0, ((0, 16), (1, 2))),
        "span_q": draw_span_q(jax.random.fold_in(seeds[18], 71), 0),
        "span_k": bell_draw(seeds[3], (SPAN, KVH * HD), 1.0, 6.0, ((0, 16), (1, 2))),
        "span_v": bell_draw(seeds[4], (SPAN, KVH * HD), 1.0, 6.0, ((0, 16), (1, 2))),
        "span_frames": jnp.searchsorted(jnp.cumsum(uneven_parts(seeds[5], 8, SPAN, SPAN // 4, 2)), jnp.arange(SPAN), side="right").astype(jnp.int32),
        "action_ids": place_ends(jax.random.randint(seeds[6], (SPAN,), 0, ACTIONS), jax.random.fold_in(seeds[6], 1), 0, ACTIONS - 1).astype(jnp.int32),
        "action_table": bell_draw(seeds[7], (ACTIONS, KVH * HD), 1.0, 6.0, ((1, 2),)),
        "frame_q": draw_frame_q(jax.random.fold_in(seeds[18], 71), 0),
        "frame_k": bell_draw(seeds[9], (FRAME, KVH * HD), 1.0, 6.0, ((0, 16), (1, 2))),
        "frame_v": bell_draw(seeds[10], (FRAME, KVH * HD), 1.0, 6.0, ((0, 16), (1, 2))),
        "revealed_k": bell_draw(seeds[11], (FRAME, KVH * HD), 1.0, 6.0, ((0, 16), (1, 2))),
        "revealed_v": bell_draw(seeds[12], (FRAME, KVH * HD), 1.0, 6.0, ((0, 16), (1, 2))),
        "mask_k": bell_draw(seeds[13], (KVH * HD,), 1.0, 6.0, ((0, 2),)),
        "mask_v": bell_draw(seeds[14], (KVH * HD,), 1.0, 6.0, ((0, 2),)),
        "pass1_idx": draw_pass1_idx(jax.random.fold_in(seeds[18], 71), 0),
        "pass2_idx": draw_pass2_idx(jax.random.fold_in(seeds[18], 71), 0),
        "out_gain": jnp.clip(1.0 + 0.1 * jax.random.normal(seeds[17], (H * HD,), jnp.float32), 0.5, 1.5),
    }


def reference_attend(queries, groups):
    group_size = H // KVH
    scaling = HD ** (-0.5)

    def one_head(head):
        kv_head = head // group_size
        query_cols = lax.dynamic_slice_in_dim(queries, head * HD, HD, 1)
        logits_all = []
        for key_rows, value_rows, allowed in groups:
            key_cols = lax.dynamic_slice_in_dim(key_rows, kv_head * HD, HD, 1)
            logits = jnp.dot(query_cols, key_cols.T, preferred_element_type=jnp.float32) * scaling
            if allowed is not None:
                logits = jnp.where(allowed, logits, -1e+30)
            logits_all.append(logits)
        maxima = logits_all[0].max(axis=1)
        for logits in logits_all[1:]:
            maxima = jnp.maximum(maxima, logits.max(axis=1))
        numerator = jnp.zeros((queries.shape[0], HD), jnp.float32)
        denominator = jnp.zeros((queries.shape[0],), jnp.float32)
        for (key_rows, value_rows, allowed), logits in zip(groups, logits_all):
            weights = jnp.exp(logits - maxima[:, None])
            denominator = denominator + weights.sum(axis=1)
            value_cols = lax.dynamic_slice_in_dim(value_rows, kv_head * HD, HD, 1)
            numerator = numerator + jnp.dot(weights.astype(jnp.bfloat16), value_cols, preferred_element_type=jnp.float32)
        return numerator / denominator[:, None]
    heads_out = lax.map(one_head, jnp.arange(H, dtype=jnp.int32))
    return heads_out.transpose(1, 0, 2).reshape(queries.shape[0], H * HD)

def normalize(attended, out_gain):
    mean_sq = lax.optimization_barrier(jnp.mean(attended * attended, axis=1, keepdims=True))
    return (attended * lax.rsqrt(mean_sq + 1e-06) * out_gain[None, :]).astype(jnp.bfloat16)

def reference(cache_k, cache_v, span_q, span_k, span_v, span_frames, action_ids, action_table, frame_q, frame_k, frame_v, revealed_k, revealed_v, mask_k, mask_v, pass1_idx, pass2_idx, out_gain):
    action_rows = jnp.take(action_table, action_ids, axis=0).astype(jnp.float32)
    span_keys = (span_k.astype(jnp.float32) + action_rows).astype(jnp.bfloat16)
    positions = jnp.arange(FRAME, dtype=jnp.int32)
    in_first = jnp.any(positions[:, None] == pass1_idx[None, :], axis=1)[:, None]
    in_second = jnp.any(positions[:, None] == pass2_idx[None, :], axis=1)[:, None]
    first_keys = jnp.where(in_first, mask_k[None, :], frame_k)
    first_values = jnp.where(in_first, mask_v[None, :], frame_v)
    second_keys = jnp.where(in_second, mask_k[None, :], jnp.where(in_first, revealed_k, frame_k))
    second_values = jnp.where(in_second, mask_v[None, :], jnp.where(in_first, revealed_v, frame_v))
    allowed = span_frames[None, :] <= span_frames[:, None]
    cache_group = (cache_k, cache_v, None)
    prefill_att = reference_attend(span_q, [cache_group, (span_keys, span_v, allowed)])
    first_att = reference_attend(jnp.take(frame_q, pass1_idx, axis=0), [cache_group, (span_keys, span_v, None), (first_keys, first_values, None)])
    second_att = reference_attend(jnp.take(frame_q, pass2_idx, axis=0), [cache_group, (span_keys, span_v, None), (second_keys, second_values, None)])
    return (normalize(prefill_att, out_gain), normalize(first_att, out_gain), normalize(second_att, out_gain))
```

```python
import functools

import jax
import jax.numpy as jnp
from jax import lax
from jax.experimental import pallas as pl
from jax.experimental.pallas import tpu as pltpu
from jax.sharding import PartitionSpec as P

HD = 128
GROUP = 4
NEG = -1e30
EPS = 1e-6
F32 = jnp.float32
BF16 = jnp.bfloat16
VMEM = pltpu.VMEM


def exchange(value, axis, mask):
    pairs = [(source, source ^ mask) for source in range(lax.axis_size(axis))]
    return lax.ppermute(value, axis, pairs)


def call(kernel, name, out_shape, *operands, scratch=(), smem=(), limit=16 * 2**20):
    in_specs = [
        pl.BlockSpec(memory_space=pltpu.SMEM if i in smem else VMEM) for i in range(len(operands))
    ]
    single = not isinstance(out_shape, (list, tuple))
    out_specs = pl.BlockSpec(memory_space=VMEM)
    if not single:
        out_specs = [out_specs] * len(out_shape)
    return pl.pallas_call(
        kernel,
        out_shape=out_shape,
        in_specs=in_specs,
        out_specs=out_specs,
        scratch_shapes=list(scratch),
        compiler_params=pltpu.CompilerParams(vmem_limit_bytes=limit),
        name=name,
    )(*operands)


def prep_kernel(
    hits, table, span_k, span_v, in1, in2, fq, fk, fv, rk, rv, mk, mv, out
):
    rows = fk.shape[0]
    width = fk.shape[1]
    terms = jnp.dot(hits[...], table[...], preferred_element_type=F32)
    span_keys = span_k[...].astype(F32) + terms
    first = in1[...] > 0.0
    second = in2[...] > 0.0
    out[0:rows, :] = fq[...]

    def put(row, column, value):
        out[row : row + rows, column * width : (column + 1) * width] = value.astype(BF16)

    put(rows, 0, span_keys)
    put(rows, 1, span_v[...])
    for given, shown, token, column in ((fk, rk, mk, 0), (fv, rv, mv, 1)):
        frame = given[...].astype(F32)
        mask = token[...].astype(F32)
        put(rows, 2 + column, jnp.where(first, mask, frame))
        put(
            2 * rows,
            column,
            jnp.where(second, mask, jnp.where(first, shown[...].astype(F32), frame)),
        )
    out[2 * rows :, 2 * width :] = jnp.zeros((rows, out.shape[1] - 2 * width), BF16)


def stacked(parts):
    return jnp.concatenate([part.astype(F32) for part in parts], axis=0).astype(BF16)


def select_kernel(rows, pick, span_q, own, m1, m2, m3, out):
    given = stacked([span_q[...]] + [m[0:rows, :] for m in (own, m1, m2, m3)])
    out[...] = jnp.dot(pick[...], given, preferred_element_type=F32).astype(BF16)


def grow_kernel(spans, mine, other, out):
    a = mine[...].astype(F32)
    b = other[...].astype(F32)
    out[...] = jnp.concatenate(
        [a[:spans], b[:spans], a[spans:] + b[spans:]], axis=0
    ).astype(BF16)


def split_stats(stats):
    lane = lax.broadcasted_iota(jnp.int32, stats.shape, 1)
    stats = jnp.where(lane < 16, stats, 0.0)
    high = stats.astype(BF16).astype(F32)
    rest = stats - high
    middle = rest.astype(BF16).astype(F32)
    low = (rest - middle).astype(BF16).astype(F32)
    packed = high + pltpu.roll(middle, 16, 1) + pltpu.roll(low, 32, 1)
    return packed.astype(BF16)


def joined_stats(packed):
    packed = packed.astype(F32)
    return packed + pltpu.roll(packed, 112, 1) + pltpu.roll(packed, 96, 1)


def attention_kernel(
    heads, rows, span_rows, keep,
    perm, allowed, mine, other, k0, k1, k2, k3, v0, v1, v2, v3, m0, m1, m2, m3,
    send, kept, kept_stats, extra_k, extra_v, att,
):
    width = heads * HD
    scaling = HD ** (-0.5)
    queries = jnp.dot(
        perm[...], stacked([mine[...], other[...]]), preferred_element_type=F32
    ).astype(BF16)
    for kind, (row, column) in enumerate(
        ((span_rows, 0), (span_rows, 2), (2 * span_rows, 0))
    ):
        for place, message in enumerate((m0, m1, m2, m3)):
            at = (kind * 4 + place) * span_rows
            for target, shift in ((extra_k, 0), (extra_v, 1)):
                left = (column + shift) * width
                target[at : at + span_rows, :] = message[
                    row : row + span_rows, left : left + width
                ].astype(F32)
    extras = 12 * span_rows
    lane = lax.broadcasted_iota(jnp.int32, (rows, HD), 1)
    stats = jnp.zeros((rows, HD), F32)
    stack = GROUP if rows * GROUP <= 128 else 1
    permit = jnp.concatenate([allowed[...]] * stack, axis=0) > 0.0
    nt = (((1,), (1,)), ((), ()))
    for g in range(heads):
        columns = slice(g * HD, (g + 1) * HD)
        values = [v[:, columns] for v in (v0, v1, v2, v3)]
        values.append(extra_v[:, columns].astype(BF16))
        keys = [k[:, columns] for k in (k0, k1, k2, k3)]
        keys.append(extra_k[:, columns].astype(BF16))
        for start in range(0, GROUP, stack):
            head = g * GROUP + start
            q = jnp.concatenate(
                [queries[:, (head + i) * HD : (head + i + 1) * HD] for i in range(stack)], axis=0
            )
            scores = [
                lax.dot_general(q, key, nt, preferred_element_type=F32) * scaling for key in keys
            ]
            scores[-1] = jnp.where(permit, scores[-1], NEG)
            top = functools.reduce(
                jnp.maximum, [s.max(axis=1, keepdims=True) for s in scores]
            )
            total = jnp.zeros_like(top)
            out = jnp.zeros((rows * stack, HD), F32)
            for s, value in zip(scores, values):
                weights = jnp.exp(s - top)
                total = total + weights.sum(axis=1, keepdims=True)
                out = out + jnp.dot(
                    weights.astype(BF16), value, preferred_element_type=F32
                )
            out = out / total
            level = top + jnp.log(total)
            for i in range(stack):
                piece = slice(i * rows, (i + 1) * rows)
                att[:, (head + i) * HD : (head + i + 1) * HD] = out[piece]
                stats = jnp.where(lane == head + i, level[piece], stats)
    kept[...] = att[:keep, :]
    kept_stats[...] = stats[:keep]
    wide = heads * GROUP * HD
    send[:, :wide] = att[keep:, :].astype(BF16)
    send[:, wide:] = split_stats(stats[keep:])


def merge(heads, kept, kept_stats, got):
    wide = heads * GROUP * HD
    mine = kept_stats[...]
    theirs = joined_stats(got[:, wide:])
    top = jnp.maximum(mine, theirs)
    a = jnp.exp(mine - top)
    b = jnp.exp(theirs - top)
    total = a + b
    a = a / total
    b = b / total
    merged = []
    for h in range(heads * GROUP):
        columns = slice(h * HD, (h + 1) * HD)
        merged.append(
            kept[:, columns] * a[:, h : h + 1] + got[:, columns].astype(F32) * b[:, h : h + 1]
        )
    return merged, top + jnp.log(total)


def merge_kernel(heads, keep, kept, kept_stats, got, send, out, out_stats):
    wide = heads * GROUP * HD
    merged, stats = merge(heads, kept, kept_stats, got)
    for h, value in enumerate(merged):
        columns = slice(h * HD, (h + 1) * HD)
        out[:, columns] = value[:keep]
        send[:, columns] = value[keep:].astype(BF16)
    out_stats[...] = stats[:keep]
    send[:, wide:] = split_stats(stats[keep:])


def last_kernel(heads, kept, kept_stats, got, out, squares):
    merged, _ = merge(heads, kept, kept_stats, got)
    total = jnp.zeros_like(merged[0])
    for h, value in enumerate(merged):
        out[:, h * HD : (h + 1) * HD] = value
        total = total + value * value
    squares[...] = jnp.broadcast_to(total.sum(axis=1, keepdims=True), squares.shape)


def out_kernel(counts, columns_all, att, squares, other, gain, *outs):
    mean_sq = (squares[...] + other[...])[:, 0:1] / columns_all
    normed = att[...] * lax.rsqrt(mean_sq + EPS) * gain[...]
    at = 0
    for count, out in zip(counts, outs):
        out[...] = normed[at : at + count].astype(BF16)
        at += count


def per_device(
    cache_k,
    cache_v,
    span_q,
    span_k,
    span_v,
    span_frames,
    action_ids,
    action_table,
    frame_q,
    frame_k,
    frame_v,
    revealed_k,
    revealed_v,
    mask_k,
    mask_v,
    pass1_idx,
    pass2_idx,
    out_gain,
):
    owners = lax.axis_size("ctx")
    tp = lax.axis_size("tp")
    me = lax.axis_index("ctx")
    blocks = owners // 4
    column = me % 4
    spans = span_k.shape[0]
    frames = frame_k.shape[0]
    width = span_k.shape[1]
    q_width = span_q.shape[1]
    heads = width // HD
    n1 = pass1_idx.shape[0] // owners
    n2 = pass2_idx.shape[0] // owners
    picked = n1 + n2
    block_rows = -(-(spans + picked) // 8) * 8
    rows = blocks * block_rows

    bits = [1 << b for b in range(2, owners.bit_length() - 1)][::-1]
    masks = [0]
    for bit in bits:
        masks = masks + [m ^ bit for m in masks]

    own_pos = me * frames + jnp.arange(frames, dtype=jnp.int32)
    in_first = jnp.any(own_pos[:, None] == pass1_idx[None, :], axis=1)[:, None].astype(F32)
    in_second = jnp.any(own_pos[:, None] == pass2_idx[None, :], axis=1)[:, None].astype(F32)
    actions = jnp.arange(action_table.shape[0], dtype=jnp.int32)
    hits = (action_ids[:, None] == actions[None, :]).astype(BF16)
    message = call(
        prep_kernel,
        "plane_message",
        jax.ShapeDtypeStruct((3 * frames, q_width), BF16),
        hits, action_table, span_k, span_v, in_first, in_second, frame_q,
        frame_k, frame_v, revealed_k, revealed_v, mask_k[None, :], mask_v[None, :],
    )

    m2 = exchange(message, "ctx", 2)
    m3 = exchange(message, "ctx", 3)
    m1 = exchange(message, "ctx", 1)
    k2 = exchange(cache_k, "ctx", 2)
    v2 = exchange(cache_v, "ctx", 2)
    k1 = exchange(cache_k, "ctx", 1)
    v1 = exchange(cache_v, "ctx", 1)
    k3 = exchange(k2, "ctx", 1)
    v3 = exchange(v2, "ctx", 1)

    want1 = lax.dynamic_index_in_dim(pass1_idx.reshape(blocks, 4, n1), column, 1, False)
    want2 = lax.dynamic_index_in_dim(pass2_idx.reshape(blocks, 4, n2), column, 1, False)
    wanted = jnp.concatenate([want1, want2], axis=1).reshape(-1)
    plane = jnp.arange(4, dtype=jnp.int32) ^ me
    plane_frames = (plane[:, None] * frames + jnp.arange(frames, dtype=jnp.int32)).reshape(-1)
    pick = jnp.concatenate(
        [
            jnp.eye(spans, spans + 4 * frames, dtype=BF16),
            jnp.concatenate(
                [
                    jnp.zeros((blocks * picked, spans), BF16),
                    (wanted[:, None] == plane_frames[None, :]).astype(BF16),
                ],
                axis=1,
            ),
        ],
        axis=0,
    )
    state = call(
        functools.partial(select_kernel, frames),
        "column_queries",
        jax.ShapeDtypeStruct((spans + blocks * picked, q_width), BF16),
        pick, span_q, message, m1, m2, m3,
    )
    held = spans
    for bit in bits[:-1]:
        other = exchange(state, "ctx", bit)
        state = call(
            functools.partial(grow_kernel, held),
            "more_queries",
            jax.ShapeDtypeStruct((state.shape[0] + held, q_width), BF16),
            state, other,
        )
        held = 2 * held
    other = exchange(state, "ctx", bits[-1])

    depth = state.shape[0]
    own_block = me // 4
    at_block = jnp.arange(rows, dtype=jnp.int32) // block_rows
    at_row = jnp.arange(rows, dtype=jnp.int32) % block_rows
    mask_of = jnp.repeat(jnp.array(masks, jnp.int32), block_rows)
    half = blocks // 2
    span_at = jnp.where(
        at_block < half, at_block * spans, depth + (at_block - half) * spans
    ) + at_row
    pick_at = held + (own_block ^ (mask_of // 4)) * picked + at_row - spans
    is_span = at_row < spans
    is_pick = (at_row >= spans) & (at_row < spans + picked)
    source = jnp.arange(2 * depth, dtype=jnp.int32)[None, :]
    perm = (
        (is_span[:, None] & (source == span_at[:, None]))
        | (is_pick[:, None] & (source % depth == pick_at[:, None]))
    ).astype(BF16)

    key_frames = span_frames[
        (plane[:, None] * spans + jnp.arange(spans, dtype=jnp.int32)).reshape(-1)
    ]
    row_frames = span_frames[jnp.where(is_span, (me ^ mask_of) * spans + at_row, 0)]
    sees_span = ~is_span[:, None] | (key_frames[None, :] <= row_frames[:, None])
    sees_first = jnp.broadcast_to(
        (is_pick & (at_row < spans + n1))[:, None], (rows, 4 * frames)
    )
    sees_second = jnp.broadcast_to(
        (is_pick & (at_row >= spans + n1))[:, None], (rows, 4 * frames)
    )
    allowed = jnp.concatenate([sees_span, sees_first, sees_second], axis=1).astype(F32)

    keep = rows // 2
    packed = q_width + HD
    send, kept, stats = call(
        functools.partial(attention_kernel, heads, rows, spans, keep),
        "plane_attention",
        [
            jax.ShapeDtypeStruct((keep, packed), BF16),
            jax.ShapeDtypeStruct((keep, q_width), F32),
            jax.ShapeDtypeStruct((keep, HD), F32),
        ],
        perm, allowed, state, other,
        cache_k, k1, k2, k3, cache_v, v1, v2, v3, message, m1, m2, m3,
        scratch=[
            pltpu.VMEM((12 * spans, width), F32),
            pltpu.VMEM((12 * spans, width), F32),
            pltpu.VMEM((rows, q_width), F32),
        ],
        limit=(16 if blocks <= 4 else 40) * 2**20,
    )
    for bit in bits[:0:-1]:
        got = exchange(send, "ctx", bit)
        keep = keep // 2
        send, kept, stats = call(
            functools.partial(merge_kernel, heads, keep),
            "merge_partials",
            [
                jax.ShapeDtypeStruct((keep, packed), BF16),
                jax.ShapeDtypeStruct((keep, q_width), F32),
                jax.ShapeDtypeStruct((keep, HD), F32),
            ],
            kept, stats, got,
        )
    got = exchange(send, "ctx", bits[0])
    att, squares = call(
        functools.partial(last_kernel, heads),
        "merge_last",
        [
            jax.ShapeDtypeStruct((block_rows, q_width), F32),
            jax.ShapeDtypeStruct((block_rows, HD), F32),
        ],
        kept, stats, got,
    )
    other_squares = exchange(squares, "tp", 1)
    counts = (spans, n1, n2)
    return tuple(
        call(
            functools.partial(out_kernel, counts, float(tp * q_width)),
            "normalize",
            [jax.ShapeDtypeStruct((count, q_width), BF16) for count in counts],
            att, squares, other_squares, out_gain[None, :],
        )
    )


def solution(mesh):
    in_specs = (
        P("ctx", "tp"),
        P("ctx", "tp"),
        P("ctx", "tp"),
        P("ctx", "tp"),
        P("ctx", "tp"),
        P(),
        P("ctx"),
        P(None, "tp"),
        P("ctx", "tp"),
        P("ctx", "tp"),
        P("ctx", "tp"),
        P("ctx", "tp"),
        P("ctx", "tp"),
        P("tp"),
        P("tp"),
        P(),
        P(),
        P("tp"),
    )
    out_specs = (P("ctx", "tp"), P("ctx", "tp"), P("ctx", "tp"))
    return jax.shard_map(
        per_device, mesh=mesh, in_specs=in_specs, out_specs=out_specs, check_vma=False
    )
```

```python
import functools

import jax
import jax.numpy as jnp
from jax import lax
from jax.experimental import pallas as pl
from jax.experimental.pallas import tpu as pltpu
from jax.sharding import PartitionSpec as P

HD = 128
GROUP = 4
NEG = -1e30
EPS = 1e-6
F32 = jnp.float32
BF16 = jnp.bfloat16
VMEM = pltpu.VMEM
PLAN_LIMIT = 60 * 2**20


def exchange(value, axis, mask):
    pairs = [(source, source ^ mask) for source in range(lax.axis_size(axis))]
    return lax.ppermute(value, axis, pairs)


def call(
    kernel, name, out_shape, *operands, scratch=(), places=None, aliases=None, out_any=(), limit=16 * 2**20
):
    places = places or {}
    in_specs = [
        pl.BlockSpec(memory_space=places.get(i, VMEM)) for i in range(len(operands))
    ]
    single = not isinstance(out_shape, (list, tuple))
    out_specs = pl.BlockSpec(memory_space=VMEM)
    aliases = aliases or {}
    if not single:
        moved = {*aliases.values(), *out_any}
        out_specs = [
            pl.BlockSpec(memory_space=pl.ANY if i in moved else VMEM)
            for i in range(len(out_shape))
        ]
    return pl.pallas_call(
        kernel,
        out_shape=out_shape,
        in_specs=in_specs,
        out_specs=out_specs,
        scratch_shapes=list(scratch),
        input_output_aliases=aliases,
        compiler_params=pltpu.CompilerParams(vmem_limit_bytes=limit),
        name=name,
    )(*operands)


def iota(shape, dim):
    return lax.broadcasted_iota(jnp.int32, shape, dim)


def split_index(index, size):
    whole = ((index.astype(F32) + 0.5) * (1.0 / size)).astype(jnp.int32)
    return whole, index - whole * size


def at_lane(row, index):
    lanes = iota((index.shape[0], row.shape[1]), 1)
    return jnp.where(lanes == index, row.astype(F32), 0.0).sum(axis=1, keepdims=True)


def plan_kernel(
    sizes, place,
    ids_h, idx1_h, idx2_h, span_frames_h, table_h, span_k_h, span_v_h,
    fk_h, fv_h, rk_h, rv_h, mk_h, mv_h, cache_k_h, cache_v_h,
    k0, v0, perm, allowed, *scratch,
):
    spans, frames, n1, n2, blocks, block_rows, mask_bits = sizes
    given = (ids_h, idx1_h, idx2_h, span_frames_h, table_h, span_k_h, span_v_h,
             fk_h, fv_h, rk_h, rv_h, mk_h, mv_h, cache_k_h, cache_v_h)
    held, (whole_k, whole_v, sems) = scratch[:-3], scratch[-3:]
    cached = cache_k_h.shape[0]
    extras = whole_k.shape[0] - cached
    staged = (whole_k.at[0:cached], whole_v.at[0:cached])
    copies = [
        pltpu.make_async_copy(source, target, sems.at[i])
        for i, (source, target) in enumerate(zip(given, (*held, *staged)))
    ]
    for copy in copies:
        copy.start()
    for copy in copies[:-2]:
        copy.wait()
    ids, idx1, idx2, span_frames, table, span_k, span_v, fk, fv, rk, rv, mk, mv = held
    me = place[0]
    own_block = me >> 2
    picked = n1 + n2

    hits = at_lane(ids[...], iota((spans, 1), 0))
    hits = (iota((spans, table.shape[0]), 1).astype(F32) == hits).astype(BF16)
    terms = jnp.dot(hits, table[...], preferred_element_type=F32)
    position = me * frames + iota((frames, 1), 0)

    def listed(idx):
        same = jnp.where(idx[...] == position, 1.0, 0.0)
        return same.sum(axis=1, keepdims=True) > 0.0

    first = listed(idx1)
    second = listed(idx2)
    sets = [span_k[...].astype(F32) + terms, span_v[...].astype(F32)]
    shown = []
    for frame, revealed, token in ((fk, rk, mk), (fv, rv, mv)):
        frame = frame[...].astype(F32)
        token = token[...].astype(F32).reshape(1, -1)
        sets.append(jnp.where(first, token, frame))
        shown.append(
            jnp.where(second, token, jnp.where(first, revealed[...].astype(F32), frame))
        )
    sets += shown
    for i, (whole, target) in enumerate(((whole_k, k0), (whole_v, v0))):
        rest = jnp.zeros((extras - 3 * spans, whole.shape[1]), F32)
        whole[cached:, :] = jnp.concatenate(sets[i::2] + [rest], axis=0).astype(BF16)
        copies[i - 2].wait()
    out_copies = [
        pltpu.make_async_copy(whole, target, sems.at[len(given) + i])
        for i, (whole, target) in enumerate(((whole_k, k0), (whole_v, v0)))
    ]
    for copy in out_copies:
        copy.start()

    rows, both = perm.shape
    depth = both // 2
    row = iota((rows, 1), 0)
    block, at = split_index(row, block_rows)
    mask = jnp.zeros_like(block)
    for i in range(mask_bits):
        mask = mask + (((block >> i) & 1) << (mask_bits + 1 - i))
    half = blocks // 2
    span_at = block * spans + at + jnp.where(block < half, 0, depth - half * spans)
    pick_at = depth - blocks * picked + (own_block ^ (mask >> 2)) * picked + at - spans
    is_span = at < spans
    is_pick = (at >= spans) & (at < spans + picked)
    lane = iota((1, both), 1)
    same = (is_span & (lane == span_at)) | (
        is_pick & ((lane == pick_at) | (lane == pick_at + depth))
    )
    perm[...] = jnp.where(same, 1.0, 0.0).astype(BF16)

    count = allowed.shape[1]
    lane = iota((1, count), 1)
    member, key_at = split_index(lane, extras)
    key = jnp.where(key_at < spans, (member ^ me) * spans + key_at, -1)
    total = span_frames.shape[1]
    numbers = jnp.broadcast_to(span_frames[...].astype(F32), (8, total)).astype(BF16)
    key_hits = jnp.where(iota((total, 1), 0) == key, 1.0, 0.0).astype(BF16)
    key_frames = jnp.dot(numbers, key_hits, preferred_element_type=F32)[0:1]
    row_frames = at_lane(span_frames[...], jnp.where(is_span, (me ^ mask) * spans + at, -1))
    sees = (key_at < spans) & ((at >= spans) | (key_frames <= row_frames))
    in_first = (key_at >= spans) & (key_at < 2 * spans)
    in_second = (key_at >= 2 * spans) & (key_at < 3 * spans)
    sees = sees | (in_first & is_pick & (at < spans + n1))
    sees = sees | (in_second & is_pick & (at >= spans + n1))
    allowed[...] = jnp.where(sees, 1.0, 0.0)
    for copy in out_copies:
        copy.wait()


def stacked(parts):
    return jnp.concatenate([part.astype(F32) for part in parts], axis=0).astype(BF16)


def select_kernel(sizes, place, idx1, idx2, span_q, own, q1, q2, q3, out):
    spans, frames, n1, n2 = sizes
    me = place[0]
    column = me & 3
    picked = n1 + n2
    shape = (out.shape[0], spans + 4 * frames)
    row = iota((shape[0], 1), 0)
    block, at = split_index(jnp.maximum(row - spans, 0), picked)
    owner = block * 4 + column
    wanted = jnp.where(
        at < n1,
        at_lane(idx1[...], owner * n1 + at),
        at_lane(idx2[...], owner * n2 + at - n1),
    )
    lane = iota((1, shape[1]), 1)
    member, at = split_index(jnp.maximum(lane - spans, 0), frames)
    position = ((member ^ me) * frames + at).astype(F32)
    chosen = jnp.where((lane >= spans) & (row >= spans) & (wanted == position), 1.0, 0.0)
    copied = jnp.where((row < spans) & (lane == row), 1.0, 0.0)
    pick = (chosen + copied).astype(BF16)
    given = stacked([q[...] for q in (span_q, own, q1, q2, q3)])
    out[...] = jnp.dot(pick, given, preferred_element_type=F32).astype(BF16)


def tie_kernel(*_):
    pass


def tie(*arrays):
    count = len(arrays)
    return call(
        tie_kernel,
        "arrived",
        [jax.ShapeDtypeStruct(array.shape, array.dtype) for array in arrays],
        *arrays,
        places={i: pl.ANY for i in range(count)},
        aliases={i: i for i in range(count)},
    )


def grow_kernel(spans, mine, other, out):
    a = mine[...].astype(F32)
    b = other[...].astype(F32)
    out[...] = jnp.concatenate(
        [a[:spans], b[:spans], a[spans:] + b[spans:]], axis=0
    ).astype(BF16)


def split_stats(stats):
    lane = lax.broadcasted_iota(jnp.int32, stats.shape, 1)
    stats = jnp.where(lane < 16, stats, 0.0)
    high = stats.astype(BF16).astype(F32)
    rest = stats - high
    middle = rest.astype(BF16).astype(F32)
    low = (rest - middle).astype(BF16).astype(F32)
    packed = high + pltpu.roll(middle, 16, 1) + pltpu.roll(low, 32, 1)
    return packed.astype(BF16)


def joined_stats(packed):
    packed = packed.astype(F32)
    return packed + pltpu.roll(packed, 112, 1) + pltpu.roll(packed, 96, 1)


def softmax_parts(heads, rows, queries, permit, key_refs, value_refs, extras, visit, before=None):
    scaling = HD ** (-0.5)
    cached = key_refs[0].shape[0] - extras
    stack = GROUP if rows * GROUP <= 128 else 1
    permit = jnp.concatenate([permit] * stack, axis=0) > 0.0
    nt = (((1,), (1,)), ((), ()))
    for g in range(heads):
        columns = slice(g * HD, (g + 1) * HD)
        keys = [ref[0:cached, columns] for ref in key_refs]
        keys.append(jnp.concatenate([ref[cached:, columns] for ref in key_refs], axis=0))
        values = [ref[0:cached, columns] for ref in value_refs]
        values.append(jnp.concatenate([ref[cached:, columns] for ref in value_refs], axis=0))
        for head in range(g * GROUP, (g + 1) * GROUP, stack):
            q = jnp.concatenate(
                [queries[:, (head + i) * HD : (head + i + 1) * HD] for i in range(stack)], axis=0
            )
            scores = [
                lax.dot_general(q, key, nt, preferred_element_type=F32) * scaling for key in keys
            ]
            scores[-1] = jnp.where(permit, scores[-1], NEG)
            top = functools.reduce(jnp.maximum, scores[:-1]).max(axis=1, keepdims=True)
            top = jnp.maximum(top, scores[-1].max(axis=1, keepdims=True))
            if before is not None:
                earlier = [ref[head * rows : (head + stack) * rows, :] for ref in before]
                top = jnp.maximum(top, earlier[0][:, 0:1])
            weights = [jnp.exp(s - top) for s in scores]
            total = functools.reduce(jnp.add, weights[:-1]).sum(axis=1, keepdims=True)
            total = total + weights[-1].sum(axis=1, keepdims=True)
            out = functools.reduce(
                jnp.add,
                [
                    jnp.dot(w.astype(BF16), value, preferred_element_type=F32)
                    for w, value in zip(weights, values)
                ],
            )
            top = jnp.broadcast_to(top, out.shape)
            if before is not None:
                scale = jnp.exp(earlier[0] - top)
                total = earlier[1] * scale + total
                out = earlier[2] * scale + out
            visit(head, stack, top, jnp.broadcast_to(total, out.shape), out)


def first_attention_kernel(
    heads, rows, extras, perm, allowed, mine, other, k0, k1, k2, v0, v1, v2,
    queries, tops, totals, sums,
):
    queries[...] = jnp.dot(
        perm[...], stacked([mine[...], other[...]]), preferred_element_type=F32
    ).astype(BF16)

    def visit(head, stack, top, total, out):
        place = slice(head * rows, (head + stack) * rows)
        tops[place, :] = top
        totals[place, :] = total
        sums[place, :] = out

    softmax_parts(
        heads, rows, queries, allowed[:, 0 : 3 * extras], (k0, k1, k2), (v0, v1, v2), extras, visit
    )


def second_attention_kernel(
    heads, rows, extras, keep, queries, allowed, tops, totals, sums, k3, v3,
    send, kept, kept_stats,
):
    wide = heads * GROUP * HD
    lane = iota((rows, HD), 1)
    held = [jnp.zeros((rows, HD), F32)]

    def visit(head, stack, top, total, out):
        out = out / total
        level = top + jnp.log(total)
        for i in range(stack):
            first = i * rows
            columns = slice((head + i) * HD, (head + i + 1) * HD)
            kept[:, columns] = out[first : first + keep]
            send[:, columns] = out[first + keep : first + rows].astype(BF16)
            held[0] = jnp.where(lane == head + i, level[first : first + rows], held[0])

    softmax_parts(
        heads, rows, queries, allowed[:, 3 * extras : 4 * extras], (k3,), (v3,), extras, visit,
        (tops, totals, sums),
    )
    kept_stats[...] = held[0][:keep]
    send[:, wide:] = split_stats(held[0][keep:])


def merge(heads, kept, kept_stats, got):
    wide = heads * GROUP * HD
    mine = kept_stats[...]
    theirs = joined_stats(got[:, wide:])
    top = jnp.maximum(mine, theirs)
    a = jnp.exp(mine - top)
    b = jnp.exp(theirs - top)
    total = a + b
    a = a / total
    b = b / total
    merged = []
    for h in range(heads * GROUP):
        columns = slice(h * HD, (h + 1) * HD)
        merged.append(
            kept[:, columns] * a[:, h : h + 1] + got[:, columns].astype(F32) * b[:, h : h + 1]
        )
    return merged, top + jnp.log(total)


def merge_kernel(heads, keep, kept, kept_stats, got, send, out, out_stats):
    wide = heads * GROUP * HD
    merged, stats = merge(heads, kept, kept_stats, got)
    for h, value in enumerate(merged):
        columns = slice(h * HD, (h + 1) * HD)
        out[:, columns] = value[:keep]
        send[:, columns] = value[keep:].astype(BF16)
    out_stats[...] = stats[:keep]
    send[:, wide:] = split_stats(stats[keep:])


def last_kernel(heads, kept, kept_stats, got, out, squares):
    merged, _ = merge(heads, kept, kept_stats, got)
    total = jnp.zeros_like(merged[0])
    for h, value in enumerate(merged):
        out[:, h * HD : (h + 1) * HD] = value
        total = total + value * value
    squares[...] = jnp.broadcast_to(total.sum(axis=1, keepdims=True), squares.shape)


def out_kernel(counts, columns_all, att, squares, other, gain, *outs):
    mean_sq = (squares[...] + other[...])[:, 0:1] / columns_all
    normed = att[...] * lax.rsqrt(mean_sq + EPS) * gain[...]
    at = 0
    for count, out in zip(counts, outs):
        out[...] = normed[at : at + count].astype(BF16)
        at += count


def per_device(
    cache_k,
    cache_v,
    span_q,
    span_k,
    span_v,
    span_frames,
    action_ids,
    action_table,
    frame_q,
    frame_k,
    frame_v,
    revealed_k,
    revealed_v,
    mask_k,
    mask_v,
    pass1_idx,
    pass2_idx,
    out_gain,
):
    owners = lax.axis_size("ctx")
    tp = lax.axis_size("tp")
    me = lax.axis_index("ctx")
    blocks = owners // 4
    spans = span_k.shape[0]
    frames = frame_k.shape[0]
    width = span_k.shape[1]
    q_width = span_q.shape[1]
    heads = width // HD
    n1 = pass1_idx.shape[0] // owners
    n2 = pass2_idx.shape[0] // owners
    picked = n1 + n2
    block_rows = -(-(spans + picked) // 8) * 8
    rows = blocks * block_rows

    bits = [1 << b for b in range(2, owners.bit_length() - 1)][::-1]

    depth = (blocks // 2) * spans + blocks * picked
    extras = -(-3 * spans // 16) * 16

    q2 = exchange(frame_q, "ctx", 2)
    q3 = exchange(frame_q, "ctx", 3)
    q1 = exchange(frame_q, "ctx", 1)
    small = (
        action_ids[None, :], pass1_idx[None, :], pass2_idx[None, :], span_frames[None, :],
        action_table, span_k, span_v, frame_k, frame_v, revealed_k, revealed_v,
        mask_k, mask_v,
    )
    sizes = (spans, frames, n1, n2, blocks, block_rows, len(bits))
    keys = cache_k.shape[0] + extras
    place = me.reshape(1)
    k0, v0, perm, allowed = call(
        functools.partial(plan_kernel, sizes),
        "plane_keys",
        [
            jax.ShapeDtypeStruct((keys, width), BF16),
            jax.ShapeDtypeStruct((keys, width), BF16),
            jax.ShapeDtypeStruct((rows, 2 * depth), BF16),
            jax.ShapeDtypeStruct((rows, 4 * extras), F32),
        ],
        place, *small, cache_k, cache_v,
        places={0: pltpu.SMEM, **{i + 1: pl.ANY for i in range(len(small) + 2)}},
        out_any=(0, 1),
        scratch=[pltpu.VMEM(array.shape, array.dtype) for array in small]
        + [pltpu.VMEM((keys, width), BF16)] * 2
        + [pltpu.SemaphoreType.DMA((len(small) + 4,))],
        limit=PLAN_LIMIT,
    )
    q1, q2, q3, k0, v0 = tie(q1, q2, q3, k0, v0)
    k2 = exchange(k0, "ctx", 2)
    v2 = exchange(v0, "ctx", 2)
    k1 = exchange(k0, "ctx", 1)
    v1 = exchange(v0, "ctx", 1)

    state = call(
        functools.partial(select_kernel, (spans, frames, n1, n2)),
        "column_queries",
        jax.ShapeDtypeStruct((spans + blocks * picked, q_width), BF16),
        place, pass1_idx[None, :], pass2_idx[None, :], span_q, frame_q, q1, q2, q3,
        places={0: pltpu.SMEM},
    )
    held = spans
    for bit in bits[:-1]:
        other = exchange(state, "ctx", bit)
        state = call(
            functools.partial(grow_kernel, held),
            "more_queries",
            jax.ShapeDtypeStruct((state.shape[0] + held, q_width), BF16),
            state, other,
        )
        held = 2 * held
    other = exchange(state, "ctx", bits[-1])
    other, k2, v2 = tie(other, k2, v2)
    k3 = exchange(k2, "ctx", 1)
    v3 = exchange(v2, "ctx", 1)

    keep = rows // 2
    packed = q_width + HD
    limit = (16 if blocks <= 4 else 40) * 2**20
    queries, *before = call(
        functools.partial(first_attention_kernel, heads, rows, extras),
        "plane_attention",
        [
            jax.ShapeDtypeStruct((rows, q_width), BF16),
            *[jax.ShapeDtypeStruct((rows * q_width // HD, HD), F32)] * 3,
        ],
        perm, allowed, state, other, k0, k1, k2, v0, v1, v2,
        limit=limit,
    )
    send, kept, stats = call(
        functools.partial(second_attention_kernel, heads, rows, extras, keep),
        "rest_attention",
        [
            jax.ShapeDtypeStruct((keep, packed), BF16),
            jax.ShapeDtypeStruct((keep, q_width), F32),
            jax.ShapeDtypeStruct((keep, HD), F32),
        ],
        queries, allowed, *before, k3, v3,
        limit=limit,
    )
    for bit in bits[:0:-1]:
        got = exchange(send, "ctx", bit)
        keep = keep // 2
        send, kept, stats = call(
            functools.partial(merge_kernel, heads, keep),
            "merge_partials",
            [
                jax.ShapeDtypeStruct((keep, packed), BF16),
                jax.ShapeDtypeStruct((keep, q_width), F32),
                jax.ShapeDtypeStruct((keep, HD), F32),
            ],
            kept, stats, got,
        )
    got = exchange(send, "ctx", bits[0])
    att, squares = call(
        functools.partial(last_kernel, heads),
        "merge_last",
        [
            jax.ShapeDtypeStruct((block_rows, q_width), F32),
            jax.ShapeDtypeStruct((block_rows, HD), F32),
        ],
        kept, stats, got,
    )
    other_squares = exchange(squares, "tp", 1)
    counts = (spans, n1, n2)
    return tuple(
        call(
            functools.partial(out_kernel, counts, float(tp * q_width)),
            "normalize",
            [jax.ShapeDtypeStruct((count, q_width), BF16) for count in counts],
            att, squares, other_squares, out_gain[None, :],
        )
    )


def solution(mesh):
    in_specs = (
        P("ctx", "tp"),
        P("ctx", "tp"),
        P("ctx", "tp"),
        P("ctx", "tp"),
        P("ctx", "tp"),
        P(),
        P("ctx"),
        P(None, "tp"),
        P("ctx", "tp"),
        P("ctx", "tp"),
        P("ctx", "tp"),
        P("ctx", "tp"),
        P("ctx", "tp"),
        P("tp"),
        P("tp"),
        P(),
        P(),
        P("tp"),
    )
    out_specs = (P("ctx", "tp"), P("ctx", "tp"), P("ctx", "tp"))
    return jax.shard_map(
        per_device, mesh=mesh, in_specs=in_specs, out_specs=out_specs, check_vma=False
    )
```

```python
import functools

import jax
import jax.numpy as jnp
from jax import lax
from jax.experimental import pallas as pl
from jax.experimental.pallas import tpu as pltpu
from jax.sharding import PartitionSpec as P

HD = 128
GROUP = 4
NEG = -1e30
EPS = 1e-6
F32 = jnp.float32
BF16 = jnp.bfloat16
VMEM = pltpu.VMEM
PLAN_LIMIT = 59 * 2**20


def exchange(value, axis, mask):
    pairs = [(source, source ^ mask) for source in range(lax.axis_size(axis))]
    return lax.ppermute(value, axis, pairs)


def call(
    kernel, name, out_shape, *operands, scratch=(), places=None, aliases=None, out_any=(), limit=16 * 2**20
):
    places = places or {}
    in_specs = [
        pl.BlockSpec(memory_space=places.get(i, VMEM)) for i in range(len(operands))
    ]
    single = not isinstance(out_shape, (list, tuple))
    out_specs = pl.BlockSpec(memory_space=VMEM)
    aliases = aliases or {}
    if not single:
        moved = {*aliases.values(), *out_any}
        out_specs = [
            pl.BlockSpec(memory_space=pl.ANY if i in moved else VMEM)
            for i in range(len(out_shape))
        ]
    return pl.pallas_call(
        kernel,
        out_shape=out_shape,
        in_specs=in_specs,
        out_specs=out_specs,
        scratch_shapes=list(scratch),
        input_output_aliases=aliases,
        compiler_params=pltpu.CompilerParams(vmem_limit_bytes=limit),
        name=name,
    )(*operands)


def iota(shape, dim):
    return lax.broadcasted_iota(jnp.int32, shape, dim)


def split_index(index, size):
    whole = ((index.astype(F32) + 0.5) * (1.0 / size)).astype(jnp.int32)
    return whole, index - whole * size


def at_lane(row, index):
    lanes = iota((index.shape[0], row.shape[1]), 1)
    return jnp.where(lanes == index, row.astype(F32), 0.0).sum(axis=1, keepdims=True)


def parity(index, count):
    total = jnp.zeros_like(index)
    for i in range(count):
        total = total ^ (index >> i)
    return total & 1


def fetch(given, held, sems):
    copies = [
        pltpu.make_async_copy(source, target, sems.at[i])
        for i, (source, target) in enumerate(zip(given, held))
    ]
    for copy in copies:
        copy.start()
    return copies


def keys_kernel(
    sizes, place,
    ids_h, idx1_h, idx2_h, table_h, span_k_h, span_v_h,
    fk_h, fv_h, rk_h, rv_h, mk_h, mv_h, cache_v_h,
    values, extra, *scratch,
):
    spans, frames = sizes
    given = (ids_h, idx1_h, idx2_h, table_h, span_k_h, span_v_h,
             fk_h, fv_h, rk_h, rv_h, mk_h, mv_h, cache_v_h)
    held, sems = scratch[:-1], scratch[-1]
    cached = cache_v_h.shape[0]
    copies = fetch(given, (*held, values.at[0:cached]), sems)
    for copy in copies[:-1]:
        copy.wait()
    ids, idx1, idx2, table, span_k, span_v, fk, fv, rk, rv, mk, mv = held
    me = place[0]

    hits = at_lane(ids[...], iota((spans, 1), 0))
    hits = (iota((spans, table.shape[0]), 1).astype(F32) == hits).astype(BF16)
    terms = jnp.dot(hits, table[...], preferred_element_type=F32)
    position = me * frames + iota((frames, 1), 0)

    def listed(idx):
        same = jnp.where(idx[...] == position, 1.0, 0.0)
        return same.sum(axis=1, keepdims=True) > 0.0

    first = listed(idx1)
    second = listed(idx2)
    sets = [span_k[...].astype(F32) + terms, span_v[...].astype(F32)]
    shown = []
    for frame, revealed, token in ((fk, rk, mk), (fv, rv, mv)):
        frame = frame[...].astype(F32)
        token = token[...].astype(F32).reshape(1, -1)
        sets.append(jnp.where(first, token, frame))
        shown.append(
            jnp.where(second, token, jnp.where(first, revealed[...].astype(F32), frame))
        )
    sets += shown
    half = extra.shape[0] // 2
    rest = jnp.zeros((half - 3 * spans, extra.shape[1]), F32)
    parts = jnp.concatenate([*sets[0::2], rest, *sets[1::2], rest], axis=0).astype(BF16)
    extra[...] = parts
    values[cached:, :] = parts
    copies[-1].wait()


def plan_kernel(sizes, place, span_frames, perm, allowed):
    spans, n1, n2, blocks, block_rows, mask_bits, extras = sizes
    me = place[0]
    own_block = me >> 2
    picked = n1 + n2

    rows, both = perm.shape
    depth = both // 2
    row = iota((rows, 1), 0)
    block, at = split_index(row, block_rows)
    mask = parity(block, mask_bits)
    for i in range(mask_bits):
        mask = mask + (((block >> i) & 1) << (mask_bits + 1 - i))
    half = blocks // 2
    span_at = block * spans + at + jnp.where(block < half, 0, depth - half * spans)
    pick_at = depth - blocks * picked + (own_block ^ (mask >> 2)) * picked + at - spans
    is_span = at < spans
    is_pick = (at >= spans) & (at < spans + picked)
    lane = iota((1, both), 1)
    same = (is_span & (lane == span_at)) | (
        is_pick & ((lane == pick_at) | (lane == pick_at + depth))
    )
    perm[...] = jnp.where(same, 1.0, 0.0).astype(BF16)

    count = allowed.shape[1]
    lane = iota((1, count), 1)
    member, key_at = split_index(lane, extras)
    key = jnp.where(key_at < spans, (member ^ me) * spans + key_at, -1)
    total = span_frames.shape[1]
    numbers = jnp.broadcast_to(span_frames[...].astype(F32), (8, total)).astype(BF16)
    key_hits = jnp.where(iota((total, 1), 0) == key, 1.0, 0.0).astype(BF16)
    key_frames = jnp.dot(numbers, key_hits, preferred_element_type=F32)[0:1]
    row_frames = at_lane(span_frames[...], jnp.where(is_span, (me ^ mask) * spans + at, -1))
    sees = (key_at < spans) & ((at >= spans) | (key_frames <= row_frames))
    in_first = (key_at >= spans) & (key_at < 2 * spans)
    in_second = (key_at >= 2 * spans) & (key_at < 3 * spans)
    sees = sees | (in_first & is_pick & (at < spans + n1))
    sees = sees | (in_second & is_pick & (at >= spans + n1))
    allowed[...] = jnp.where(sees, 1.0, 0.0)


def stacked(parts):
    return jnp.concatenate([part.astype(F32) for part in parts], axis=0).astype(BF16)


def select_kernel(sizes, place, idx1, idx2, span_q, own, q1, q2, q3, out):
    spans, frames, n1, n2, mask_bits = sizes
    me = place[0]
    column = (me & 3) ^ parity(me >> 2, mask_bits)
    picked = n1 + n2
    shape = (out.shape[0], spans + 4 * frames)
    row = iota((shape[0], 1), 0)
    block, at = split_index(jnp.maximum(row - spans, 0), picked)
    owner = block * 4 + (column ^ parity(block, mask_bits))
    wanted = jnp.where(
        at < n1,
        at_lane(idx1[...], owner * n1 + at),
        at_lane(idx2[...], owner * n2 + at - n1),
    )
    lane = iota((1, shape[1]), 1)
    member, at = split_index(jnp.maximum(lane - spans, 0), frames)
    position = ((member ^ me) * frames + at).astype(F32)
    chosen = jnp.where((lane >= spans) & (row >= spans) & (wanted == position), 1.0, 0.0)
    copied = jnp.where((row < spans) & (lane == row), 1.0, 0.0)
    pick = (chosen + copied).astype(BF16)
    given = stacked([q[...] for q in (span_q, own, q1, q2, q3)])
    out[...] = jnp.dot(pick, given, preferred_element_type=F32).astype(BF16)


def tie_kernel(*_):
    pass


def stage_kernel(*refs):
    refs[-1][...] = refs[len(refs) // 2 - 1][...]


def tie(*arrays):
    count = len(arrays)
    return call(
        tie_kernel,
        "arrived",
        [jax.ShapeDtypeStruct(array.shape, array.dtype) for array in arrays],
        *arrays,
        places={i: pl.ANY for i in range(count)},
        aliases={i: i for i in range(count)},
    )


def grow_kernel(spans, mine, other, _, out, __):
    a = mine[...].astype(F32)
    b = other[...].astype(F32)
    out[...] = jnp.concatenate(
        [a[:spans], b[:spans], a[spans:] + b[spans:]], axis=0
    ).astype(BF16)


def split_stats(stats):
    lane = lax.broadcasted_iota(jnp.int32, stats.shape, 1)
    stats = jnp.where(lane < 16, stats, 0.0)
    high = stats.astype(BF16).astype(F32)
    rest = stats - high
    middle = rest.astype(BF16).astype(F32)
    low = (rest - middle).astype(BF16).astype(F32)
    packed = high + pltpu.roll(middle, 16, 1) + pltpu.roll(low, 32, 1)
    return packed.astype(BF16)


def joined_stats(packed):
    packed = packed.astype(F32)
    return packed + pltpu.roll(packed, 112, 1) + pltpu.roll(packed, 96, 1)


def attention_kernel(
    heads, rows, extras, keep,
    perm, allowed, mine, other, k0, k1, k2, k3, v0, v1, v2, v3, extra,
    send, kept, kept_stats,
):
    queries = jnp.dot(
        perm[...], stacked([mine[...], other[...]]), preferred_element_type=F32
    ).astype(BF16)
    wide = heads * GROUP * HD
    scaling = HD ** (-0.5)
    cached = k0.shape[0]
    stack = GROUP if rows * GROUP <= 128 else 1
    permit = jnp.concatenate([allowed[...]] * stack, axis=0) > 0.0
    nt = (((1,), (1,)), ((), ()))
    lane = iota((rows, HD), 1)
    stats = jnp.zeros((rows, HD), F32)

    def blocks_of(refs, g, first):
        columns = slice(g * HD, (g + 1) * HD)
        parts = [ref[0:cached, columns] for ref in refs]
        rest = [extra[first : first + extras, columns]]
        at = cached + first
        rest += [ref[at : at + extras, columns] for ref in (v1, v2, v3)]
        parts.append(jnp.concatenate(rest, axis=0))
        return parts

    def scores_of(head):
        q = jnp.concatenate(
            [queries[:, (head + i) * HD : (head + i + 1) * HD] for i in range(stack)], axis=0
        )
        scores = [
            lax.dot_general(q, key, nt, preferred_element_type=F32) * scaling
            for key in blocks_of((k0, k1, k2, k3), head // GROUP, 0)
        ]
        scores[-1] = jnp.where(permit, scores[-1], NEG)
        return scores

    def weights_of(scores):
        top = functools.reduce(jnp.maximum, scores[:-1]).max(axis=1, keepdims=True)
        top = jnp.maximum(top, scores[-1].max(axis=1, keepdims=True))
        weights = [jnp.exp(s - top) for s in scores]
        total = functools.reduce(jnp.add, weights[:-1]).sum(axis=1, keepdims=True)
        return top, total + weights[-1].sum(axis=1, keepdims=True), weights

    steps = range(0, heads * GROUP, stack)
    for first in range(0, len(steps), 2):
        group = steps[first : first + 2]
        scored = [scores_of(head) for head in group]
        weighed = [weights_of(scores) for scores in scored]
        for head, (top, total, weights) in zip(group, weighed):
            out = functools.reduce(
                jnp.add,
                [
                    jnp.dot(w.astype(BF16), value, preferred_element_type=F32)
                    for w, value in zip(
                        weights, blocks_of((v0, v1, v2, v3), head // GROUP, extras)
                    )
                ],
            )
            out = out / total
            level = top + jnp.log(total)
            for i in range(stack):
                at = i * rows
                columns = slice((head + i) * HD, (head + i + 1) * HD)
                kept[:, columns] = out[at : at + keep]
                send[:, columns] = out[at + keep : at + rows].astype(BF16)
                stats = jnp.where(lane == head + i, level[at : at + rows], stats)
    kept_stats[...] = stats[:keep]
    send[:, wide:] = split_stats(stats[keep:])


def merge(heads, kept, kept_stats, got):
    wide = heads * GROUP * HD
    mine = kept_stats[...]
    theirs = joined_stats(got[:, wide:])
    top = jnp.maximum(mine, theirs)
    a = jnp.exp(mine - top)
    b = jnp.exp(theirs - top)
    total = a + b
    a = a / total
    b = b / total
    merged = []
    for h in range(heads * GROUP):
        columns = slice(h * HD, (h + 1) * HD)
        merged.append(
            kept[:, columns] * a[:, h : h + 1] + got[:, columns].astype(F32) * b[:, h : h + 1]
        )
    return merged, top + jnp.log(total)


def merge_kernel(heads, keep, kept, kept_stats, got, send, out, out_stats):
    wide = heads * GROUP * HD
    merged, stats = merge(heads, kept, kept_stats, got)
    for h, value in enumerate(merged):
        columns = slice(h * HD, (h + 1) * HD)
        out[:, columns] = value[:keep]
        send[:, columns] = value[keep:].astype(BF16)
    out_stats[...] = stats[:keep]
    send[:, wide:] = split_stats(stats[keep:])


def last_kernel(heads, kept, kept_stats, got, out, squares):
    merged, _ = merge(heads, kept, kept_stats, got)
    total = jnp.zeros_like(merged[0])
    for h, value in enumerate(merged):
        out[:, h * HD : (h + 1) * HD] = value
        total = total + value * value
    squares[...] = jnp.broadcast_to(total.sum(axis=1, keepdims=True), squares.shape)


def out_kernel(counts, columns_all, att, squares, other, gain, *outs):
    mean_sq = (squares[...] + other[...])[:, 0:1] / columns_all
    normed = att[...] * lax.rsqrt(mean_sq + EPS) * gain[...]
    at = 0
    for count, out in zip(counts, outs):
        out[...] = normed[at : at + count].astype(BF16)
        at += count


def per_device(
    cache_k,
    cache_v,
    span_q,
    span_k,
    span_v,
    span_frames,
    action_ids,
    action_table,
    frame_q,
    frame_k,
    frame_v,
    revealed_k,
    revealed_v,
    mask_k,
    mask_v,
    pass1_idx,
    pass2_idx,
    out_gain,
):
    owners = lax.axis_size("ctx")
    tp = lax.axis_size("tp")
    me = lax.axis_index("ctx")
    blocks = owners // 4
    spans = span_k.shape[0]
    frames = frame_k.shape[0]
    width = span_k.shape[1]
    q_width = span_q.shape[1]
    heads = width // HD
    n1 = pass1_idx.shape[0] // owners
    n2 = pass2_idx.shape[0] // owners
    picked = n1 + n2
    block_rows = -(-(spans + picked) // 8) * 8
    rows = blocks * block_rows

    bits = [(1 << b) + 1 for b in range(2, owners.bit_length() - 1)][::-1]

    depth = (blocks // 2) * spans + blocks * picked
    extras = -(-3 * spans // 16) * 16

    q3 = exchange(frame_q, "ctx", 3)
    q1 = exchange(frame_q, "ctx", 1)
    small = (
        action_ids[None, :], pass1_idx[None, :], pass2_idx[None, :],
        action_table, span_k, span_v, frame_k, frame_v, revealed_k, revealed_v,
        mask_k, mask_v,
    )
    place = me.reshape(1)
    values, extra = call(
        functools.partial(keys_kernel, (spans, frames)),
        "plane_values",
        [
            jax.ShapeDtypeStruct((cache_v.shape[0] + 2 * extras, width), BF16),
            jax.ShapeDtypeStruct((2 * extras, width), BF16),
        ],
        place, *small, cache_v,
        places={0: pltpu.SMEM, **{i + 1: pl.ANY for i in range(len(small) + 1)}},
        scratch=[pltpu.VMEM(array.shape, array.dtype) for array in small]
        + [pltpu.SemaphoreType.DMA((len(small) + 1,))],
        limit=PLAN_LIMIT,
    )
    moved = (q1, q3, values)
    q1, q3, values, k0 = call(
        stage_kernel,
        "plane_queries_arrived",
        [jax.ShapeDtypeStruct(array.shape, array.dtype) for array in (*moved, cache_k)],
        *moved, cache_k,
        places={i: pl.ANY for i in range(len(moved))},
        aliases={i: i for i in range(len(moved))},
    )
    q2 = exchange(q3, "ctx", 1)
    k3 = exchange(k0, "ctx", 3)
    v3 = exchange(values, "ctx", 3)
    k1 = exchange(k0, "ctx", 1)
    v1 = exchange(values, "ctx", 1)

    state = call(
        functools.partial(select_kernel, (spans, frames, n1, n2, len(bits))),
        "column_queries",
        jax.ShapeDtypeStruct((spans + blocks * picked, q_width), BF16),
        place, pass1_idx[None, :], pass2_idx[None, :], span_q, frame_q, q1, q2, q3,
        places={0: pltpu.SMEM},
    )

    held = spans
    for bit in bits[:-1]:
        other = exchange(state, "ctx", bit)
        state, k3 = call(
            functools.partial(grow_kernel, held),
            "more_queries",
            [
                jax.ShapeDtypeStruct((state.shape[0] + held, q_width), BF16),
                jax.ShapeDtypeStruct(k3.shape, BF16),
            ],
            state, other, k3,
            places={2: pl.ANY},
            aliases={2: 1},
        )
        held = 2 * held
    other = exchange(state, "ctx", bits[-1])
    k2 = exchange(k3, "ctx", 1)
    other, v3 = tie(other, v3)
    v2 = exchange(v3, "ctx", 1)

    perm, allowed = call(
        functools.partial(plan_kernel, (spans, n1, n2, blocks, block_rows, len(bits), extras)),
        "row_plan",
        [
            jax.ShapeDtypeStruct((rows, 2 * depth), BF16),
            jax.ShapeDtypeStruct((rows, 4 * extras), F32),
        ],
        place, span_frames[None, :],
        places={0: pltpu.SMEM},
    )
    keep = rows // 2
    packed = q_width + HD
    send, kept, stats = call(
        functools.partial(attention_kernel, heads, rows, extras, keep),
        "plane_attention",
        [
            jax.ShapeDtypeStruct((keep, packed), BF16),
            jax.ShapeDtypeStruct((keep, q_width), F32),
            jax.ShapeDtypeStruct((keep, HD), F32),
        ],
        perm, allowed, state, other, k0, k1, k2, k3, cache_v, v1, v2, v3, extra,
        limit=(16 if blocks <= 4 else 40) * 2**20,
    )
    for bit in bits[:0:-1]:
        got = exchange(send, "ctx", bit)
        keep = keep // 2
        send, kept, stats = call(
            functools.partial(merge_kernel, heads, keep),
            "merge_partials",
            [
                jax.ShapeDtypeStruct((keep, packed), BF16),
                jax.ShapeDtypeStruct((keep, q_width), F32),
                jax.ShapeDtypeStruct((keep, HD), F32),
            ],
            kept, stats, got,
        )
    got = exchange(send, "ctx", bits[0])
    att, squares = call(
        functools.partial(last_kernel, heads),
        "merge_last",
        [
            jax.ShapeDtypeStruct((block_rows, q_width), F32),
            jax.ShapeDtypeStruct((block_rows, HD), F32),
        ],
        kept, stats, got,
    )
    other_squares = exchange(squares, "tp", 1)
    counts = (spans, n1, n2)
    return tuple(
        call(
            functools.partial(out_kernel, counts, float(tp * q_width)),
            "normalize",
            [jax.ShapeDtypeStruct((count, q_width), BF16) for count in counts],
            att, squares, other_squares, out_gain[None, :],
        )
    )


def solution(mesh):
    in_specs = (
        P("ctx", "tp"),
        P("ctx", "tp"),
        P("ctx", "tp"),
        P("ctx", "tp"),
        P("ctx", "tp"),
        P(),
        P("ctx"),
        P(None, "tp"),
        P("ctx", "tp"),
        P("ctx", "tp"),
        P("ctx", "tp"),
        P("ctx", "tp"),
        P("ctx", "tp"),
        P("tp"),
        P("tp"),
        P(),
        P(),
        P("tp"),
    )
    out_specs = (P("ctx", "tp"), P("ctx", "tp"), P("ctx", "tp"))
    return jax.shard_map(
        per_device, mesh=mesh, in_specs=in_specs, out_specs=out_specs, check_vma=False
    )
```

```python
import functools

import jax
import jax.numpy as jnp
from jax import lax
from jax.experimental import pallas as pl
from jax.experimental.pallas import tpu as pltpu
from jax.sharding import PartitionSpec as P

HD = 128
GROUP = 4
NEG = -1e30
EPS = 1e-6
F32 = jnp.float32
BF16 = jnp.bfloat16
VMEM = pltpu.VMEM
PLAN_LIMIT = 59 * 2**20
PLAN_BYTES = 108000000
PLAN_FLOPS = 34500000000


def exchange(value, axis, mask):
    pairs = [(source, source ^ mask) for source in range(lax.axis_size(axis))]
    return lax.ppermute(value, axis, pairs)


def call(
    kernel, name, out_shape, *operands, scratch=(), places=None, cost=None, aliases=None, out_any=(), limit=16 * 2**20
):
    places = places or {}
    in_specs = [
        pl.BlockSpec(memory_space=places.get(i, VMEM)) for i in range(len(operands))
    ]
    single = not isinstance(out_shape, (list, tuple))
    out_specs = pl.BlockSpec(memory_space=VMEM)
    aliases = aliases or {}
    if not single:
        moved = {*aliases.values(), *out_any}
        out_specs = [
            pl.BlockSpec(memory_space=pl.ANY if i in moved else VMEM)
            for i in range(len(out_shape))
        ]
    return pl.pallas_call(
        kernel,
        out_shape=out_shape,
        in_specs=in_specs,
        out_specs=out_specs,
        scratch_shapes=list(scratch),
        input_output_aliases=aliases,
        compiler_params=pltpu.CompilerParams(vmem_limit_bytes=limit),
        cost_estimate=cost,
        name=name,
    )(*operands)


def iota(shape, dim):
    return lax.broadcasted_iota(jnp.int32, shape, dim)


def split_index(index, size):
    whole = ((index.astype(F32) + 0.5) * (1.0 / size)).astype(jnp.int32)
    return whole, index - whole * size


def at_lane(row, index):
    lanes = iota((index.shape[0], row.shape[1]), 1)
    return jnp.where(lanes == index, row.astype(F32), 0.0).sum(axis=1, keepdims=True)


def parity(index, count):
    total = jnp.zeros_like(index)
    for i in range(count):
        total = total ^ (index >> i)
    return total & 1


def fetch(given, held, sems):
    copies = [
        pltpu.make_async_copy(source, target, sems.at[i])
        for i, (source, target) in enumerate(zip(given, held))
    ]
    for copy in copies:
        copy.start()
    return copies


def keys_kernel(
    sizes, place,
    ids_h, idx1_h, idx2_h, table_h, span_k_h, span_v_h,
    fk_h, fv_h, rk_h, rv_h, mk_h, mv_h, cache_v_h,
    values, extra, done, *scratch,
):
    spans, frames = sizes
    given = (ids_h, idx1_h, idx2_h, table_h, span_k_h, span_v_h,
             fk_h, fv_h, rk_h, rv_h, mk_h, mv_h, cache_v_h)
    held, sems = scratch[:-1], scratch[-1]
    cached = cache_v_h.shape[0]
    copies = fetch(given, (*held, values.at[0:cached]), sems)
    for copy in copies[:-1]:
        copy.wait()
    ids, idx1, idx2, table, span_k, span_v, fk, fv, rk, rv, mk, mv = held
    me = place[0]

    hits = at_lane(ids[...], iota((spans, 1), 0))
    hits = (iota((spans, table.shape[0]), 1).astype(F32) == hits).astype(BF16)
    terms = jnp.dot(hits, table[...], preferred_element_type=F32)
    position = me * frames + iota((frames, 1), 0)

    def listed(idx):
        same = jnp.where(idx[...] == position, 1.0, 0.0)
        return same.sum(axis=1, keepdims=True) > 0.0

    first = listed(idx1)
    second = listed(idx2)
    sets = [span_k[...].astype(F32) + terms, span_v[...].astype(F32)]
    shown = []
    for frame, revealed, token in ((fk, rk, mk), (fv, rv, mv)):
        frame = frame[...].astype(F32)
        token = token[...].astype(F32).reshape(1, -1)
        sets.append(jnp.where(first, token, frame))
        shown.append(
            jnp.where(second, token, jnp.where(first, revealed[...].astype(F32), frame))
        )
    sets += shown
    half = extra.shape[0] // 2
    rest = jnp.zeros((half - 3 * spans, extra.shape[1]), F32)
    parts = jnp.concatenate([*sets[0::2], rest, *sets[1::2], rest], axis=0).astype(BF16)
    extra[...] = parts
    values[cached:, :] = parts
    done[...] = jnp.zeros(done.shape, F32)
    copies[-1].wait()


def plan_kernel(sizes, place, span_frames, perm, allowed):
    spans, n1, n2, blocks, block_rows, mask_bits, extras = sizes
    me = place[0]
    own_block = me >> 2
    picked = n1 + n2

    rows, both = perm.shape
    depth = both // 2
    row = iota((rows, 1), 0)
    block, at = split_index(row, block_rows)
    mask = parity(block, mask_bits)
    for i in range(mask_bits):
        mask = mask + (((block >> i) & 1) << (mask_bits + 1 - i))
    half = blocks // 2
    span_at = block * spans + at + jnp.where(block < half, 0, depth - half * spans)
    pick_at = depth - blocks * picked + (own_block ^ (mask >> 2)) * picked + at - spans
    is_span = at < spans
    is_pick = (at >= spans) & (at < spans + picked)
    lane = iota((1, both), 1)
    same = (is_span & (lane == span_at)) | (
        is_pick & ((lane == pick_at) | (lane == pick_at + depth))
    )
    perm[...] = jnp.where(same, 1.0, 0.0).astype(BF16)

    count = allowed.shape[1]
    lane = iota((1, count), 1)
    member, key_at = split_index(lane, extras)
    key = jnp.where(key_at < spans, (member ^ me) * spans + key_at, -1)
    total = span_frames.shape[1]
    numbers = jnp.broadcast_to(span_frames[...].astype(F32), (8, total)).astype(BF16)
    key_hits = jnp.where(iota((total, 1), 0) == key, 1.0, 0.0).astype(BF16)
    key_frames = jnp.dot(numbers, key_hits, preferred_element_type=F32)[0:1]
    row_frames = at_lane(span_frames[...], jnp.where(is_span, (me ^ mask) * spans + at, -1))
    sees = (key_at < spans) & ((at >= spans) | (key_frames <= row_frames))
    in_first = (key_at >= spans) & (key_at < 2 * spans)
    in_second = (key_at >= 2 * spans) & (key_at < 3 * spans)
    sees = sees | (in_first & is_pick & (at < spans + n1))
    sees = sees | (in_second & is_pick & (at >= spans + n1))
    allowed[...] = jnp.where(sees, 1.0, 0.0)


def stacked(parts):
    return jnp.concatenate([part.astype(F32) for part in parts], axis=0).astype(BF16)


def select_kernel(sizes, place, idx1, idx2, span_q, pair, other, out):
    spans, frames, n1, n2, mask_bits = sizes
    me = place[0]
    column = (me & 3) ^ parity(me >> 2, mask_bits)
    picked = n1 + n2
    shape = (out.shape[0], spans + 4 * frames)
    row = iota((shape[0], 1), 0)
    block, at = split_index(jnp.maximum(row - spans, 0), picked)
    owner = block * 4 + (column ^ parity(block, mask_bits))
    wanted = jnp.where(
        at < n1,
        at_lane(idx1[...], owner * n1 + at),
        at_lane(idx2[...], owner * n2 + at - n1),
    )
    lane = iota((1, shape[1]), 1)
    member, at = split_index(jnp.maximum(lane - spans, 0), frames)
    position = ((member ^ me) * frames + at).astype(F32)
    chosen = jnp.where((lane >= spans) & (row >= spans) & (wanted == position), 1.0, 0.0)
    copied = jnp.where((row < spans) & (lane == row), 1.0, 0.0)
    pick = (chosen + copied).astype(BF16)
    given = stacked([span_q[...], pair[0:frames], other[...], pair[frames:]])
    out[...] = jnp.dot(pick, given, preferred_element_type=F32).astype(BF16)


def tie_kernel(*_):
    pass


def listed_kernel(_, idx1, idx2, out1, out2):
    out1[...] = idx1[...]
    out2[...] = idx2[...]


def stage_kernel(cached, spans, mine, other, copied, pair, copied_spans):
    copied[...] = cached[...]
    copied_spans[...] = spans[...]
    pair[...] = stacked([mine[...], other[...]])


def tie(*arrays):
    count = len(arrays)
    return call(
        tie_kernel,
        "arrived",
        [jax.ShapeDtypeStruct(array.shape, array.dtype) for array in arrays],
        *arrays,
        places={i: pl.ANY for i in range(count)},
        aliases={i: i for i in range(count)},
    )


def grow_kernel(spans, mine, other, _, __, out, *___):
    a = mine[...].astype(F32)
    b = other[...].astype(F32)
    out[...] = jnp.concatenate(
        [a[:spans], b[:spans], a[spans:] + b[spans:]], axis=0
    ).astype(BF16)


def split_stats(stats):
    lane = lax.broadcasted_iota(jnp.int32, stats.shape, 1)
    stats = jnp.where(lane < 16, stats, 0.0)
    high = stats.astype(BF16).astype(F32)
    rest = stats - high
    middle = rest.astype(BF16).astype(F32)
    low = (rest - middle).astype(BF16).astype(F32)
    packed = high + pltpu.roll(middle, 16, 1) + pltpu.roll(low, 32, 1)
    return packed.astype(BF16)


def joined_stats(packed):
    packed = packed.astype(F32)
    return packed + pltpu.roll(packed, 112, 1) + pltpu.roll(packed, 96, 1)


def attention_kernel(
    heads, rows, extras, keep,
    perm, allowed, mine, other, k0, k1, k2, k3, v0, v1, v2, v3, extra,
    send, kept, kept_stats,
):
    queries = jnp.dot(
        perm[...], stacked([mine[...], other[...]]), preferred_element_type=F32
    ).astype(BF16)
    wide = heads * GROUP * HD
    scaling = HD ** (-0.5)
    cached = k0.shape[0]
    stack = GROUP if rows * GROUP <= 128 else 1
    permit = jnp.concatenate([allowed[...]] * stack, axis=0) > 0.0
    nt = (((1,), (1,)), ((), ()))
    lane = iota((rows, HD), 1)
    stats = jnp.zeros((rows, HD), F32)

    def blocks_of(refs, g, first):
        columns = slice(g * HD, (g + 1) * HD)
        parts = [ref[0:cached, columns] for ref in refs]
        rest = [extra[first : first + extras, columns]]
        at = cached + first
        rest += [ref[at : at + extras, columns] for ref in (v1, v2, v3)]
        parts.append(jnp.concatenate(rest, axis=0))
        return parts

    def scores_of(head):
        q = jnp.concatenate(
            [queries[:, (head + i) * HD : (head + i + 1) * HD] for i in range(stack)], axis=0
        )
        scores = [
            lax.dot_general(q, key, nt, preferred_element_type=F32) * scaling
            for key in blocks_of((k0, k1, k2, k3), head // GROUP, 0)
        ]
        scores[-1] = jnp.where(permit, scores[-1], NEG)
        return scores

    def weights_of(scores):
        top = functools.reduce(jnp.maximum, scores[:-1]).max(axis=1, keepdims=True)
        top = jnp.maximum(top, scores[-1].max(axis=1, keepdims=True))
        weights = [jnp.exp(s - top) for s in scores]
        total = functools.reduce(jnp.add, weights[:-1]).sum(axis=1, keepdims=True)
        return top, total + weights[-1].sum(axis=1, keepdims=True), weights

    steps = range(0, heads * GROUP, stack)
    for first in range(0, len(steps), 2):
        group = steps[first : first + 2]
        scored = [scores_of(head) for head in group]
        weighed = [weights_of(scores) for scores in scored]
        for head, (top, total, weights) in zip(group, weighed):
            out = functools.reduce(
                jnp.add,
                [
                    jnp.dot(w.astype(BF16), value, preferred_element_type=F32)
                    for w, value in zip(
                        weights, blocks_of((v0, v1, v2, v3), head // GROUP, extras)
                    )
                ],
            )
            out = out / total
            level = top + jnp.log(total)
            for i in range(stack):
                at = i * rows
                columns = slice((head + i) * HD, (head + i + 1) * HD)
                kept[:, columns] = out[at : at + keep]
                send[:, columns] = out[at + keep : at + rows].astype(BF16)
                stats = jnp.where(lane == head + i, level[at : at + rows], stats)
    kept_stats[...] = stats[:keep]
    send[:, wide:] = split_stats(stats[keep:])


def merge(heads, kept, kept_stats, got):
    wide = heads * GROUP * HD
    mine = kept_stats[...]
    theirs = joined_stats(got[:, wide:])
    top = jnp.maximum(mine, theirs)
    a = jnp.exp(mine - top)
    b = jnp.exp(theirs - top)
    total = a + b
    a = a / total
    b = b / total
    merged = []
    for h in range(heads * GROUP):
        columns = slice(h * HD, (h + 1) * HD)
        merged.append(
            kept[:, columns] * a[:, h : h + 1] + got[:, columns].astype(F32) * b[:, h : h + 1]
        )
    return merged, top + jnp.log(total)


def merge_kernel(heads, keep, kept, kept_stats, got, send, out, out_stats):
    wide = heads * GROUP * HD
    merged, stats = merge(heads, kept, kept_stats, got)
    for h, value in enumerate(merged):
        columns = slice(h * HD, (h + 1) * HD)
        out[:, columns] = value[:keep]
        send[:, columns] = value[keep:].astype(BF16)
    out_stats[...] = stats[:keep]
    send[:, wide:] = split_stats(stats[keep:])


def last_kernel(heads, kept, kept_stats, got, out, squares):
    merged, _ = merge(heads, kept, kept_stats, got)
    total = jnp.zeros_like(merged[0])
    for h, value in enumerate(merged):
        out[:, h * HD : (h + 1) * HD] = value
        total = total + value * value
    squares[...] = jnp.broadcast_to(total.sum(axis=1, keepdims=True), squares.shape)


def out_kernel(counts, columns_all, att, squares, other, gain, *outs):
    mean_sq = (squares[...] + other[...])[:, 0:1] / columns_all
    normed = att[...] * lax.rsqrt(mean_sq + EPS) * gain[...]
    at = 0
    for count, out in zip(counts, outs):
        out[...] = normed[at : at + count].astype(BF16)
        at += count


def per_device(
    cache_k,
    cache_v,
    span_q,
    span_k,
    span_v,
    span_frames,
    action_ids,
    action_table,
    frame_q,
    frame_k,
    frame_v,
    revealed_k,
    revealed_v,
    mask_k,
    mask_v,
    pass1_idx,
    pass2_idx,
    out_gain,
):
    owners = lax.axis_size("ctx")
    tp = lax.axis_size("tp")
    me = lax.axis_index("ctx")
    blocks = owners // 4
    spans = span_k.shape[0]
    frames = frame_k.shape[0]
    width = span_k.shape[1]
    q_width = span_q.shape[1]
    heads = width // HD
    n1 = pass1_idx.shape[0] // owners
    n2 = pass2_idx.shape[0] // owners
    picked = n1 + n2
    block_rows = -(-(spans + picked) // 8) * 8
    rows = blocks * block_rows

    bits = [(1 << b) + 1 for b in range(2, owners.bit_length() - 1)][::-1]

    depth = (blocks // 2) * spans + blocks * picked
    extras = -(-3 * spans // 16) * 16

    q3 = exchange(frame_q, "ctx", 3)
    small = (
        action_ids[None, :], pass1_idx[None, :], pass2_idx[None, :],
        action_table, span_k, span_v, frame_k, frame_v, revealed_k, revealed_v,
        mask_k, mask_v,
    )
    place = me.reshape(1)
    values, extra, token = call(
        functools.partial(keys_kernel, (spans, frames)),
        "plane_values",
        [
            jax.ShapeDtypeStruct((cache_v.shape[0] + 2 * extras, width), BF16),
            jax.ShapeDtypeStruct((2 * extras, width), BF16),
            jax.ShapeDtypeStruct((8, HD), F32),
        ],
        place, *small, cache_v,
        places={0: pltpu.SMEM, **{i + 1: pl.ANY for i in range(len(small) + 1)}},
        scratch=[pltpu.VMEM(array.shape, array.dtype) for array in small]
        + [pltpu.SemaphoreType.DMA((len(small) + 1,))],
        limit=PLAN_LIMIT,
        cost=pl.CostEstimate(flops=PLAN_FLOPS, bytes_accessed=PLAN_BYTES, transcendentals=0),
    )
    k0, chip, own_spans = call(
        stage_kernel,
        "queries_arrived",
        [
            jax.ShapeDtypeStruct(cache_k.shape, BF16),
            jax.ShapeDtypeStruct((2 * frames, q_width), BF16),
            jax.ShapeDtypeStruct(span_q.shape, BF16),
        ],
        cache_k, span_q, frame_q, q3,
    )
    other_chip = exchange(chip, "ctx", 1)
    idx1, idx2 = call(
        listed_kernel,
        "listed",
        [jax.ShapeDtypeStruct((1, idx.shape[0]), idx.dtype) for idx in (pass1_idx, pass2_idx)],
        token, pass1_idx[None, :], pass2_idx[None, :],
        places={0: pl.ANY},
        cost=pl.CostEstimate(flops=PLAN_FLOPS, bytes_accessed=PLAN_BYTES, transcendentals=0),
    )
    k3 = exchange(cache_k, "ctx", 3)
    v3 = exchange(values, "ctx", 3)
    k1 = exchange(k0, "ctx", 1)
    v1 = exchange(values, "ctx", 1)

    state = call(
        functools.partial(select_kernel, (spans, frames, n1, n2, len(bits))),
        "column_queries",
        jax.ShapeDtypeStruct((spans + blocks * picked, q_width), BF16),
        place, idx1, idx2, own_spans, chip, other_chip,
        places={0: pltpu.SMEM},
    )

    held = spans
    for bit in bits[:-1]:
        other = exchange(state, "ctx", bit)
        state, k3, k1 = call(
            functools.partial(grow_kernel, held),
            "more_queries",
            [
                jax.ShapeDtypeStruct((state.shape[0] + held, q_width), BF16),
                jax.ShapeDtypeStruct(k3.shape, BF16),
                jax.ShapeDtypeStruct(k1.shape, BF16),
            ],
            state, other, k3, k1,
            places={2: pl.ANY, 3: pl.ANY},
            aliases={2: 1, 3: 2},
        )
        held = 2 * held
    other = exchange(state, "ctx", bits[-1])
    k2 = exchange(k3, "ctx", 1)
    other, v3, k2 = tie(other, v3, k2)
    v2 = exchange(v3, "ctx", 1)

    perm, allowed = call(
        functools.partial(plan_kernel, (spans, n1, n2, blocks, block_rows, len(bits), extras)),
        "row_plan",
        [
            jax.ShapeDtypeStruct((rows, 2 * depth), BF16),
            jax.ShapeDtypeStruct((rows, 4 * extras), F32),
        ],
        place, span_frames[None, :],
        places={0: pltpu.SMEM},
    )
    keep = rows // 2
    packed = q_width + HD
    send, kept, stats = call(
        functools.partial(attention_kernel, heads, rows, extras, keep),
        "plane_attention",
        [
            jax.ShapeDtypeStruct((keep, packed), BF16),
            jax.ShapeDtypeStruct((keep, q_width), F32),
            jax.ShapeDtypeStruct((keep, HD), F32),
        ],
        perm, allowed, state, other, k0, k1, k2, k3, cache_v, v1, v2, v3, extra,
        limit=(16 if blocks <= 4 else 40) * 2**20,
    )
    for bit in bits[:0:-1]:
        got = exchange(send, "ctx", bit)
        keep = keep // 2
        send, kept, stats = call(
            functools.partial(merge_kernel, heads, keep),
            "merge_partials",
            [
                jax.ShapeDtypeStruct((keep, packed), BF16),
                jax.ShapeDtypeStruct((keep, q_width), F32),
                jax.ShapeDtypeStruct((keep, HD), F32),
            ],
            kept, stats, got,
        )
    got = exchange(send, "ctx", bits[0])
    att, squares = call(
        functools.partial(last_kernel, heads),
        "merge_last",
        [
            jax.ShapeDtypeStruct((block_rows, q_width), F32),
            jax.ShapeDtypeStruct((block_rows, HD), F32),
        ],
        kept, stats, got,
    )
    other_squares = exchange(squares, "tp", 1)
    counts = (spans, n1, n2)
    return tuple(
        call(
            functools.partial(out_kernel, counts, float(tp * q_width)),
            "normalize",
            [jax.ShapeDtypeStruct((count, q_width), BF16) for count in counts],
            att, squares, other_squares, out_gain[None, :],
        )
    )


def solution(mesh):
    in_specs = (
        P("ctx", "tp"),
        P("ctx", "tp"),
        P("ctx", "tp"),
        P("ctx", "tp"),
        P("ctx", "tp"),
        P(),
        P("ctx"),
        P(None, "tp"),
        P("ctx", "tp"),
        P("ctx", "tp"),
        P("ctx", "tp"),
        P("ctx", "tp"),
        P("ctx", "tp"),
        P("tp"),
        P("tp"),
        P(),
        P(),
        P("tp"),
    )
    out_specs = (P("ctx", "tp"), P("ctx", "tp"), P("ctx", "tp"))
    return jax.shard_map(
        per_device, mesh=mesh, in_specs=in_specs, out_specs=out_specs, check_vma=False
    )
```

```python
import functools

import jax
import jax.numpy as jnp
from jax import lax
from jax.experimental import pallas as pl
from jax.experimental.pallas import tpu as pltpu
from jax.sharding import PartitionSpec as P

HD = 128
GROUP = 4
NEG = -1e30
EPS = 1e-6
F32 = jnp.float32
BF16 = jnp.bfloat16
VMEM = pltpu.VMEM
PLAN_LIMIT = 59 * 2**20
PLAN_BYTES = 108000000
PLAN_FLOPS = 34500000000


def exchange(value, axis, mask):
    pairs = [(source, source ^ mask) for source in range(lax.axis_size(axis))]
    return lax.ppermute(value, axis, pairs)


def call(
    kernel, name, out_shape, *operands, scratch=(), places=None, cost=None, aliases=None, out_any=(), limit=16 * 2**20
):
    places = places or {}
    in_specs = [
        pl.BlockSpec(memory_space=places.get(i, VMEM)) for i in range(len(operands))
    ]
    single = not isinstance(out_shape, (list, tuple))
    out_specs = pl.BlockSpec(memory_space=VMEM)
    aliases = aliases or {}
    if not single:
        moved = {*aliases.values(), *out_any}
        out_specs = [
            pl.BlockSpec(memory_space=pl.ANY if i in moved else VMEM)
            for i in range(len(out_shape))
        ]
    return pl.pallas_call(
        kernel,
        out_shape=out_shape,
        in_specs=in_specs,
        out_specs=out_specs,
        scratch_shapes=list(scratch),
        input_output_aliases=aliases,
        compiler_params=pltpu.CompilerParams(vmem_limit_bytes=limit),
        cost_estimate=cost,
        name=name,
    )(*operands)


def iota(shape, dim):
    return lax.broadcasted_iota(jnp.int32, shape, dim)


def split_index(index, size):
    whole = ((index.astype(F32) + 0.5) * (1.0 / size)).astype(jnp.int32)
    return whole, index - whole * size


def at_lane(row, index):
    lanes = iota((index.shape[0], row.shape[1]), 1)
    return jnp.where(lanes == index, row.astype(F32), 0.0).sum(axis=1, keepdims=True)


def parity(index, count):
    total = jnp.zeros_like(index)
    for i in range(count):
        total = total ^ (index >> i)
    return total & 1


def fetch(given, held, sems):
    copies = [
        pltpu.make_async_copy(source, target, sems.at[i])
        for i, (source, target) in enumerate(zip(given, held))
    ]
    for copy in copies:
        copy.start()
    return copies


def keys_kernel(
    sizes, place,
    ids_h, idx1_h, idx2_h, table_h, span_k_h, span_v_h,
    fk_h, fv_h, rk_h, rv_h, mk_h, mv_h, cache_v_h,
    values, extra, done, *scratch,
):
    spans, frames = sizes
    given = (ids_h, idx1_h, idx2_h, table_h, span_k_h, span_v_h,
             fk_h, fv_h, rk_h, rv_h, mk_h, mv_h, cache_v_h)
    held, sems = scratch[:-1], scratch[-1]
    cached = cache_v_h.shape[0]
    copies = fetch(given, (*held, values.at[0:cached]), sems)
    for copy in copies[:-1]:
        copy.wait()
    ids, idx1, idx2, table, span_k, span_v, fk, fv, rk, rv, mk, mv = held
    me = place[0]

    hits = at_lane(ids[...], iota((spans, 1), 0))
    hits = (iota((spans, table.shape[0]), 1).astype(F32) == hits).astype(BF16)
    terms = jnp.dot(hits, table[...], preferred_element_type=F32)
    position = me * frames + iota((frames, 1), 0)

    def listed(idx):
        same = jnp.where(idx[...] == position, 1.0, 0.0)
        return same.sum(axis=1, keepdims=True) > 0.0

    first = listed(idx1)
    second = listed(idx2)
    sets = [span_k[...].astype(F32) + terms, span_v[...].astype(F32)]
    shown = []
    for frame, revealed, token in ((fk, rk, mk), (fv, rv, mv)):
        frame = frame[...].astype(F32)
        token = token[...].astype(F32).reshape(1, -1)
        sets.append(jnp.where(first, token, frame))
        shown.append(
            jnp.where(second, token, jnp.where(first, revealed[...].astype(F32), frame))
        )
    sets += shown
    half = extra.shape[0] // 2
    rest = jnp.zeros((half - 3 * spans, extra.shape[1]), F32)
    parts = jnp.concatenate([*sets[0::2], rest, *sets[1::2], rest], axis=0).astype(BF16)
    extra[...] = parts
    values[cached:, :] = parts
    done[...] = jnp.zeros(done.shape, F32)
    copies[-1].wait()


def plan_kernel(sizes, place, span_frames, perm, allowed):
    spans, n1, n2, blocks, block_rows, mask_bits, extras = sizes
    me = place[0]
    own_block = me >> 2
    picked = n1 + n2

    rows, both = perm.shape
    depth = both // 2
    row = iota((rows, 1), 0)
    block, at = split_index(row, block_rows)
    mask = parity(block, mask_bits)
    for i in range(mask_bits):
        mask = mask + (((block >> i) & 1) << (mask_bits + 1 - i))
    half = blocks // 2
    span_at = block * spans + at + jnp.where(block < half, 0, depth - half * spans)
    pick_at = depth - blocks * picked + (own_block ^ (mask >> 2)) * picked + at - spans
    is_span = at < spans
    is_pick = (at >= spans) & (at < spans + picked)
    lane = iota((1, both), 1)
    same = (is_span & (lane == span_at)) | (
        is_pick & ((lane == pick_at) | (lane == pick_at + depth))
    )
    perm[...] = jnp.where(same, 1.0, 0.0).astype(BF16)

    count = allowed.shape[1]
    lane = iota((1, count), 1)
    member, key_at = split_index(lane, extras)
    key = jnp.where(key_at < spans, (member ^ me) * spans + key_at, -1)
    total = span_frames.shape[1]
    numbers = jnp.broadcast_to(span_frames[...].astype(F32), (8, total)).astype(BF16)
    key_hits = jnp.where(iota((total, 1), 0) == key, 1.0, 0.0).astype(BF16)
    key_frames = jnp.dot(numbers, key_hits, preferred_element_type=F32)[0:1]
    row_frames = at_lane(span_frames[...], jnp.where(is_span, (me ^ mask) * spans + at, -1))
    sees = (key_at < spans) & ((at >= spans) | (key_frames <= row_frames))
    in_first = (key_at >= spans) & (key_at < 2 * spans)
    in_second = (key_at >= 2 * spans) & (key_at < 3 * spans)
    sees = sees | (in_first & is_pick & (at < spans + n1))
    sees = sees | (in_second & is_pick & (at >= spans + n1))
    allowed[...] = jnp.where(sees, 1.0, 0.0)


def stacked(parts):
    return jnp.concatenate([part.astype(F32) for part in parts], axis=0).astype(BF16)


def select_kernel(sizes, place, idx1, idx2, span_q, pair, other, out):
    spans, frames, n1, n2, mask_bits = sizes
    me = place[0]
    column = (me & 3) ^ parity(me >> 2, mask_bits)
    picked = n1 + n2
    shape = (out.shape[0], spans + 4 * frames)
    row = iota((shape[0], 1), 0)
    block, at = split_index(jnp.maximum(row - spans, 0), picked)
    owner = block * 4 + (column ^ parity(block, mask_bits))
    wanted = jnp.where(
        at < n1,
        at_lane(idx1[...], owner * n1 + at),
        at_lane(idx2[...], owner * n2 + at - n1),
    )
    lane = iota((1, shape[1]), 1)
    member, at = split_index(jnp.maximum(lane - spans, 0), frames)
    position = ((member ^ me) * frames + at).astype(F32)
    chosen = jnp.where((lane >= spans) & (row >= spans) & (wanted == position), 1.0, 0.0)
    copied = jnp.where((row < spans) & (lane == row), 1.0, 0.0)
    pick = (chosen + copied).astype(BF16)
    given = stacked([span_q[...], pair[0:frames], other[...], pair[frames:]])
    out[...] = jnp.dot(pick, given, preferred_element_type=F32).astype(BF16)


def tie_kernel(*_):
    pass


def listed_kernel(_, idx1, idx2, out1, out2):
    out1[...] = idx1[...]
    out2[...] = idx2[...]


def stage_kernel(cached, spans, mine, other, copied, pair, copied_spans):
    copied[...] = cached[...]
    copied_spans[...] = spans[...]
    pair[...] = stacked([mine[...], other[...]])


def tie(*arrays):
    count = len(arrays)
    return call(
        tie_kernel,
        "arrived",
        [jax.ShapeDtypeStruct(array.shape, array.dtype) for array in arrays],
        *arrays,
        places={i: pl.ANY for i in range(count)},
        aliases={i: i for i in range(count)},
    )


def grow_kernel(spans, mine, other, _, __, out, *___):
    a = mine[...].astype(F32)
    b = other[...].astype(F32)
    out[...] = jnp.concatenate(
        [a[:spans], b[:spans], a[spans:] + b[spans:]], axis=0
    ).astype(BF16)


def split_stats(stats):
    lane = lax.broadcasted_iota(jnp.int32, stats.shape, 1)
    stats = jnp.where(lane < 16, stats, 0.0)
    high = stats.astype(BF16).astype(F32)
    rest = stats - high
    middle = rest.astype(BF16).astype(F32)
    low = (rest - middle).astype(BF16).astype(F32)
    packed = high + pltpu.roll(middle, 16, 1) + pltpu.roll(low, 32, 1)
    return packed.astype(BF16)


def joined_stats(packed):
    packed = packed.astype(F32)
    return packed + pltpu.roll(packed, 112, 1) + pltpu.roll(packed, 96, 1)


def attention_kernel(
    heads, first_row, extras,
    perm, allowed, mine, other, k0, k1, k2, k3, v0, v1, v2, v3, extra, *outs,
):
    rows = perm.shape[0] // 2
    half = slice(first_row, first_row + rows)
    message = len(outs) == 1
    queries = jnp.dot(
        perm[half, :], stacked([mine[...], other[...]]), preferred_element_type=F32
    ).astype(BF16)
    wide = heads * GROUP * HD
    scaling = HD ** (-0.5)
    cached = k0.shape[0]
    stack = GROUP if rows * GROUP <= 128 else 1
    permit = jnp.concatenate([allowed[half, :]] * stack, axis=0) > 0.0
    nt = (((1,), (1,)), ((), ()))
    lane = iota((rows, HD), 1)
    stats = jnp.zeros((rows, HD), F32)

    def blocks_of(refs, g, first):
        columns = slice(g * HD, (g + 1) * HD)
        parts = [ref[0:cached, columns] for ref in refs]
        rest = [extra[first : first + extras, columns]]
        at = cached + first
        rest += [ref[at : at + extras, columns] for ref in (v1, v2, v3)]
        parts.append(jnp.concatenate(rest, axis=0))
        return parts

    def scores_of(head):
        q = jnp.concatenate(
            [queries[:, (head + i) * HD : (head + i + 1) * HD] for i in range(stack)], axis=0
        )
        scores = [
            lax.dot_general(q, key, nt, preferred_element_type=F32) * scaling
            for key in blocks_of((k0, k1, k2, k3), head // GROUP, 0)
        ]
        scores[-1] = jnp.where(permit, scores[-1], NEG)
        return scores

    def weights_of(scores):
        top = functools.reduce(jnp.maximum, scores[:-1]).max(axis=1, keepdims=True)
        top = jnp.maximum(top, scores[-1].max(axis=1, keepdims=True))
        weights = [jnp.exp(s - top) for s in scores]
        total = functools.reduce(jnp.add, weights[:-1]).sum(axis=1, keepdims=True)
        return top, total + weights[-1].sum(axis=1, keepdims=True), weights

    steps = range(0, heads * GROUP, stack)
    for first in range(0, len(steps), 4):
        group = steps[first : first + 4]
        scored = [scores_of(head) for head in group]
        weighed = [weights_of(scores) for scores in scored]
        for head, (top, total, weights) in zip(group, weighed):
            values = blocks_of((v0, v1, v2, v3), head // GROUP, extras)
            weights = [w.astype(BF16) for w in weights]
            out = jnp.dot(
                jnp.concatenate(weights[:-1], axis=1),
                jnp.concatenate(values[:-1], axis=0),
                preferred_element_type=F32,
            ) + jnp.dot(weights[-1], values[-1], preferred_element_type=F32)
            out = out / total
            level = top + jnp.log(total)
            for i in range(stack):
                at = i * rows
                columns = slice((head + i) * HD, (head + i + 1) * HD)
                outs[0][:, columns] = out[at : at + rows].astype(outs[0].dtype)
                stats = jnp.where(lane == head + i, level[at : at + rows], stats)
    if message:
        outs[0][:, wide:] = split_stats(stats)
    else:
        outs[1][...] = stats


def merge(heads, kept, kept_stats, got, first, rows):
    wide = heads * GROUP * HD
    half = slice(first, first + rows)
    mine = kept_stats[half, :]
    theirs = joined_stats(got[half, wide:])
    top = jnp.maximum(mine, theirs)
    a = jnp.exp(mine - top)
    b = jnp.exp(theirs - top)
    total = a + b
    a = a / total
    b = b / total
    merged = []
    for h in range(heads * GROUP):
        columns = slice(h * HD, (h + 1) * HD)
        merged.append(
            kept[half, columns] * a[:, h : h + 1]
            + got[half, columns].astype(F32) * b[:, h : h + 1]
        )
    return merged, top + jnp.log(total)


def merge_kernel(heads, first, kept, kept_stats, got, *outs):
    wide = heads * GROUP * HD
    merged, stats = merge(heads, kept, kept_stats, got, first, kept.shape[0] // 2)
    for h, value in enumerate(merged):
        outs[0][:, h * HD : (h + 1) * HD] = value.astype(outs[0].dtype)
    if len(outs) == 1:
        outs[0][:, wide:] = split_stats(stats)
    else:
        outs[1][...] = stats


def last_kernel(heads, kept, kept_stats, got, out, squares):
    merged, _ = merge(heads, kept, kept_stats, got, 0, kept.shape[0])
    total = jnp.zeros_like(merged[0])
    for h, value in enumerate(merged):
        out[:, h * HD : (h + 1) * HD] = value
        total = total + value * value
    squares[...] = jnp.broadcast_to(total.sum(axis=1, keepdims=True), squares.shape)


def out_kernel(counts, columns_all, att, squares, other, gain, *outs):
    mean_sq = (squares[...] + other[...])[:, 0:1] / columns_all
    normed = att[...] * lax.rsqrt(mean_sq + EPS) * gain[...]
    at = 0
    for count, out in zip(counts, outs):
        out[...] = normed[at : at + count].astype(BF16)
        at += count


def per_device(
    cache_k,
    cache_v,
    span_q,
    span_k,
    span_v,
    span_frames,
    action_ids,
    action_table,
    frame_q,
    frame_k,
    frame_v,
    revealed_k,
    revealed_v,
    mask_k,
    mask_v,
    pass1_idx,
    pass2_idx,
    out_gain,
):
    owners = lax.axis_size("ctx")
    tp = lax.axis_size("tp")
    me = lax.axis_index("ctx")
    blocks = owners // 4
    spans = span_k.shape[0]
    frames = frame_k.shape[0]
    width = span_k.shape[1]
    q_width = span_q.shape[1]
    heads = width // HD
    n1 = pass1_idx.shape[0] // owners
    n2 = pass2_idx.shape[0] // owners
    picked = n1 + n2
    block_rows = -(-(spans + picked) // 8) * 8
    rows = blocks * block_rows

    bits = [(1 << b) + 1 for b in range(2, owners.bit_length() - 1)][::-1]

    depth = (blocks // 2) * spans + blocks * picked
    extras = -(-3 * spans // 16) * 16

    q3 = exchange(frame_q, "ctx", 3)
    small = (
        action_ids[None, :], pass1_idx[None, :], pass2_idx[None, :],
        action_table, span_k, span_v, frame_k, frame_v, revealed_k, revealed_v,
        mask_k, mask_v,
    )
    place = me.reshape(1)
    values, extra, token = call(
        functools.partial(keys_kernel, (spans, frames)),
        "plane_values",
        [
            jax.ShapeDtypeStruct((cache_v.shape[0] + 2 * extras, width), BF16),
            jax.ShapeDtypeStruct((2 * extras, width), BF16),
            jax.ShapeDtypeStruct((8, HD), F32),
        ],
        place, *small, cache_v,
        places={0: pltpu.SMEM, **{i + 1: pl.ANY for i in range(len(small) + 1)}},
        scratch=[pltpu.VMEM(array.shape, array.dtype) for array in small]
        + [pltpu.SemaphoreType.DMA((len(small) + 1,))],
        limit=PLAN_LIMIT,
        cost=pl.CostEstimate(flops=PLAN_FLOPS, bytes_accessed=PLAN_BYTES, transcendentals=0),
    )
    k0, chip, own_spans = call(
        stage_kernel,
        "queries_arrived",
        [
            jax.ShapeDtypeStruct(cache_k.shape, BF16),
            jax.ShapeDtypeStruct((2 * frames, q_width), BF16),
            jax.ShapeDtypeStruct(span_q.shape, BF16),
        ],
        cache_k, span_q, frame_q, q3,
    )
    other_chip = exchange(chip, "ctx", 1)
    idx1, idx2 = call(
        listed_kernel,
        "listed",
        [jax.ShapeDtypeStruct((1, idx.shape[0]), idx.dtype) for idx in (pass1_idx, pass2_idx)],
        token, pass1_idx[None, :], pass2_idx[None, :],
        places={0: pl.ANY},
        cost=pl.CostEstimate(flops=PLAN_FLOPS, bytes_accessed=PLAN_BYTES, transcendentals=0),
    )
    k3 = exchange(cache_k, "ctx", 3)
    v3 = exchange(values, "ctx", 3)
    k1 = exchange(k0, "ctx", 1)
    v1 = exchange(values, "ctx", 1)

    state = call(
        functools.partial(select_kernel, (spans, frames, n1, n2, len(bits))),
        "column_queries",
        jax.ShapeDtypeStruct((spans + blocks * picked, q_width), BF16),
        place, idx1, idx2, own_spans, chip, other_chip,
        places={0: pltpu.SMEM},
    )

    held = spans
    for bit in bits[:-1]:
        other = exchange(state, "ctx", bit)
        state, k3, k1 = call(
            functools.partial(grow_kernel, held),
            "more_queries",
            [
                jax.ShapeDtypeStruct((state.shape[0] + held, q_width), BF16),
                jax.ShapeDtypeStruct(k3.shape, BF16),
                jax.ShapeDtypeStruct(k1.shape, BF16),
            ],
            state, other, k3, k1,
            places={2: pl.ANY, 3: pl.ANY},
            aliases={2: 1, 3: 2},
        )
        held = 2 * held
    other = exchange(state, "ctx", bits[-1])
    k2 = exchange(k3, "ctx", 1)
    other, v3, k2 = tie(other, v3, k2)
    v2 = exchange(v3, "ctx", 1)

    perm, allowed = call(
        functools.partial(plan_kernel, (spans, n1, n2, blocks, block_rows, len(bits), extras)),
        "row_plan",
        [
            jax.ShapeDtypeStruct((rows, 2 * depth), BF16),
            jax.ShapeDtypeStruct((rows, 4 * extras), F32),
        ],
        place, span_frames[None, :],
        places={0: pltpu.SMEM},
    )
    keep = rows // 2
    packed = q_width + HD
    given = (perm, allowed, state, other, k0, k1, k2, k3, cache_v, v1, v2, v3, extra)
    limit = (16 if blocks <= 4 else 40) * 2**20
    send = call(
        functools.partial(attention_kernel, heads, keep, extras),
        "sent_attention",
        jax.ShapeDtypeStruct((keep, packed), BF16),
        *given,
        limit=limit,
    )
    kept, stats = call(
        functools.partial(attention_kernel, heads, 0, extras),
        "kept_attention",
        [
            jax.ShapeDtypeStruct((keep, q_width), F32),
            jax.ShapeDtypeStruct((keep, HD), F32),
        ],
        *given,
        limit=limit,
    )
    for bit in bits[:0:-1]:
        got = exchange(send, "ctx", bit)
        keep = keep // 2
        given = (kept, stats, got)
        send = call(
            functools.partial(merge_kernel, heads, keep),
            "sent_partials",
            jax.ShapeDtypeStruct((keep, packed), BF16),
            *given,
        )
        kept, stats = call(
            functools.partial(merge_kernel, heads, 0),
            "kept_partials",
            [
                jax.ShapeDtypeStruct((keep, q_width), F32),
                jax.ShapeDtypeStruct((keep, HD), F32),
            ],
            *given,
        )
    got = exchange(send, "ctx", bits[0])
    att, squares = call(
        functools.partial(last_kernel, heads),
        "merge_last",
        [
            jax.ShapeDtypeStruct((block_rows, q_width), F32),
            jax.ShapeDtypeStruct((block_rows, HD), F32),
        ],
        kept, stats, got,
    )
    other_squares = exchange(squares, "tp", 1)
    counts = (spans, n1, n2)
    return tuple(
        call(
            functools.partial(out_kernel, counts, float(tp * q_width)),
            "normalize",
            [jax.ShapeDtypeStruct((count, q_width), BF16) for count in counts],
            att, squares, other_squares, out_gain[None, :],
        )
    )


def solution(mesh):
    in_specs = (
        P("ctx", "tp"),
        P("ctx", "tp"),
        P("ctx", "tp"),
        P("ctx", "tp"),
        P("ctx", "tp"),
        P(),
        P("ctx"),
        P(None, "tp"),
        P("ctx", "tp"),
        P("ctx", "tp"),
        P("ctx", "tp"),
        P("ctx", "tp"),
        P("ctx", "tp"),
        P("tp"),
        P("tp"),
        P(),
        P(),
        P("tp"),
    )
    out_specs = (P("ctx", "tp"), P("ctx", "tp"), P("ctx", "tp"))
    return jax.shard_map(
        per_device, mesh=mesh, in_specs=in_specs, out_specs=out_specs, check_vma=False
    )
```

```python
import functools

import jax
import jax.numpy as jnp
from jax import lax
from jax.experimental import pallas as pl
from jax.experimental.pallas import tpu as pltpu
from jax.sharding import PartitionSpec as P

HD = 128
GROUP = 4
NEG = -1e30
EPS = 1e-6
F32 = jnp.float32
BF16 = jnp.bfloat16
VMEM = pltpu.VMEM
PLAN_LIMIT = 59 * 2**20
PLAN_BYTES = 108000000
PLAN_FLOPS = 34500000000


def exchange(value, axis, mask):
    pairs = [(source, source ^ mask) for source in range(lax.axis_size(axis))]
    return lax.ppermute(value, axis, pairs)


def call(
    kernel, name, out_shape, *operands, scratch=(), places=None, cost=None, aliases=None, out_any=(), limit=16 * 2**20
):
    places = places or {}
    in_specs = [
        pl.BlockSpec(memory_space=places.get(i, VMEM)) for i in range(len(operands))
    ]
    single = not isinstance(out_shape, (list, tuple))
    out_specs = pl.BlockSpec(memory_space=VMEM)
    aliases = aliases or {}
    if not single:
        moved = {*aliases.values(), *out_any}
        out_specs = [
            pl.BlockSpec(memory_space=pl.ANY if i in moved else VMEM)
            for i in range(len(out_shape))
        ]
    return pl.pallas_call(
        kernel,
        out_shape=out_shape,
        in_specs=in_specs,
        out_specs=out_specs,
        scratch_shapes=list(scratch),
        input_output_aliases=aliases,
        compiler_params=pltpu.CompilerParams(vmem_limit_bytes=limit),
        cost_estimate=cost,
        name=name,
    )(*operands)


def iota(shape, dim):
    return lax.broadcasted_iota(jnp.int32, shape, dim)


def split_index(index, size):
    whole = ((index.astype(F32) + 0.5) * (1.0 / size)).astype(jnp.int32)
    return whole, index - whole * size


def at_lane(row, index):
    lanes = iota((index.shape[0], row.shape[1]), 1)
    return jnp.where(lanes == index, row.astype(F32), 0.0).sum(axis=1, keepdims=True)


def parity(index, count):
    total = jnp.zeros_like(index)
    for i in range(count):
        total = total ^ (index >> i)
    return total & 1


def fetch(given, held, sems):
    copies = [
        pltpu.make_async_copy(source, target, sems.at[i])
        for i, (source, target) in enumerate(zip(given, held))
    ]
    for copy in copies:
        copy.start()
    return copies


def keys_kernel(
    sizes, place,
    ids_h, idx1_h, idx2_h, table_h, span_k_h, span_v_h,
    fk_h, fv_h, rk_h, rv_h, mk_h, mv_h, cache_v_h,
    values, extra, done, *scratch,
):
    spans, frames = sizes
    given = (ids_h, idx1_h, idx2_h, table_h, span_k_h, span_v_h,
             fk_h, fv_h, rk_h, rv_h, mk_h, mv_h, cache_v_h)
    held, sems = scratch[:-1], scratch[-1]
    cached = cache_v_h.shape[0]
    copies = fetch(given, (*held, values.at[0:cached]), sems)
    for copy in copies[:-1]:
        copy.wait()
    ids, idx1, idx2, table, span_k, span_v, fk, fv, rk, rv, mk, mv = held
    me = place[0]

    hits = at_lane(ids[...], iota((spans, 1), 0))
    hits = (iota((spans, table.shape[0]), 1).astype(F32) == hits).astype(BF16)
    terms = jnp.dot(hits, table[...], preferred_element_type=F32)
    position = me * frames + iota((frames, 1), 0)

    def listed(idx):
        same = jnp.where(idx[...] == position, 1.0, 0.0)
        return same.sum(axis=1, keepdims=True) > 0.0

    first = listed(idx1)
    second = listed(idx2)
    sets = [span_k[...].astype(F32) + terms, span_v[...].astype(F32)]
    shown = []
    for frame, revealed, token in ((fk, rk, mk), (fv, rv, mv)):
        frame = frame[...].astype(F32)
        token = token[...].astype(F32).reshape(1, -1)
        sets.append(jnp.where(first, token, frame))
        shown.append(
            jnp.where(second, token, jnp.where(first, revealed[...].astype(F32), frame))
        )
    sets += shown
    parts = jnp.concatenate([*sets[0::2], *sets[1::2]], axis=0).astype(BF16)
    extra[...] = parts
    values[cached:, :] = parts
    done[...] = jnp.zeros(done.shape, F32)
    copies[-1].wait()


def plan_kernel(sizes, place, span_frames, perm, allowed):
    spans, n1, n2, blocks, block_rows, mask_bits, extras = sizes
    me = place[0]
    own_block = me >> 2
    picked = n1 + n2

    rows, both = perm.shape
    depth = both // 2
    row = iota((rows, 1), 0)
    block, at = split_index(row, block_rows)
    mask = parity(block, mask_bits)
    for i in range(mask_bits):
        mask = mask + (((block >> i) & 1) << (mask_bits + 1 - i))
    half = blocks // 2
    span_at = block * spans + at + jnp.where(block < half, 0, depth - half * spans)
    pick_at = depth - blocks * picked + (own_block ^ (mask >> 2)) * picked + at - spans
    is_span = at < spans
    is_pick = (at >= spans) & (at < spans + picked)
    lane = iota((1, both), 1)
    same = (is_span & (lane == span_at)) | (
        is_pick & ((lane == pick_at) | (lane == pick_at + depth))
    )
    perm[...] = jnp.where(same, 1.0, 0.0).astype(BF16)

    count = allowed.shape[1]
    lane = iota((1, count), 1)
    member, key_at = split_index(lane, extras)
    key = jnp.where(key_at < spans, (member ^ me) * spans + key_at, -1)
    total = span_frames.shape[1]
    numbers = jnp.broadcast_to(span_frames[...].astype(F32), (8, total)).astype(BF16)
    key_hits = jnp.where(iota((total, 1), 0) == key, 1.0, 0.0).astype(BF16)
    key_frames = jnp.dot(numbers, key_hits, preferred_element_type=F32)[0:1]
    row_frames = at_lane(span_frames[...], jnp.where(is_span, (me ^ mask) * spans + at, -1))
    sees = (key_at < spans) & ((at >= spans) | (key_frames <= row_frames))
    in_first = (key_at >= spans) & (key_at < 2 * spans)
    in_second = (key_at >= 2 * spans) & (key_at < 3 * spans)
    sees = sees | (in_first & is_pick & (at < spans + n1))
    sees = sees | (in_second & is_pick & (at >= spans + n1))
    allowed[...] = jnp.where(sees, 1.0, 0.0)


def stacked(parts):
    return jnp.concatenate([part.astype(F32) for part in parts], axis=0).astype(BF16)


def select_kernel(sizes, place, idx1, idx2, span_q, pair, other, out):
    spans, frames, n1, n2, mask_bits = sizes
    me = place[0]
    column = (me & 3) ^ parity(me >> 2, mask_bits)
    picked = n1 + n2
    shape = (out.shape[0], spans + 4 * frames)
    row = iota((shape[0], 1), 0)
    block, at = split_index(jnp.maximum(row - spans, 0), picked)
    owner = block * 4 + (column ^ parity(block, mask_bits))
    wanted = jnp.where(
        at < n1,
        at_lane(idx1[...], owner * n1 + at),
        at_lane(idx2[...], owner * n2 + at - n1),
    )
    lane = iota((1, shape[1]), 1)
    member, at = split_index(jnp.maximum(lane - spans, 0), frames)
    position = ((member ^ me) * frames + at).astype(F32)
    chosen = jnp.where((lane >= spans) & (row >= spans) & (wanted == position), 1.0, 0.0)
    copied = jnp.where((row < spans) & (lane == row), 1.0, 0.0)
    pick = (chosen + copied).astype(BF16)
    given = stacked([span_q[...], pair[0:frames], other[...], pair[frames:]])
    out[...] = jnp.dot(pick, given, preferred_element_type=F32).astype(BF16)


def tie_kernel(*_):
    pass


def listed_kernel(_, idx1, idx2, out1, out2):
    out1[...] = idx1[...]
    out2[...] = idx2[...]


def stage_kernel(cached, spans, mine, other, copied, pair, copied_spans):
    copied[...] = cached[...]
    copied_spans[...] = spans[...]
    pair[...] = stacked([mine[...], other[...]])


def tie(*arrays):
    count = len(arrays)
    return call(
        tie_kernel,
        "arrived",
        [jax.ShapeDtypeStruct(array.shape, array.dtype) for array in arrays],
        *arrays,
        places={i: pl.ANY for i in range(count)},
        aliases={i: i for i in range(count)},
    )


def grow_kernel(spans, mine, other, _, __, out, *___):
    a = mine[...].astype(F32)
    b = other[...].astype(F32)
    parts = [a[:spans], b[:spans], a[spans:] + b[spans:]]
    width = out.shape[1]
    pieces = [p[:, at : at + width] for at in range(0, a.shape[1], width) for p in parts]
    out[...] = jnp.concatenate(pieces, axis=0).astype(BF16)


def unfolded(state, width):
    state = state[...].astype(F32)
    count = state.shape[0] * state.shape[1] // width
    return jnp.concatenate(
        [state[at : at + count] for at in range(0, state.shape[0], count)], axis=1
    )


def split_stats(stats):
    lane = lax.broadcasted_iota(jnp.int32, stats.shape, 1)
    stats = jnp.where(lane < 16, stats, 0.0)
    high = stats.astype(BF16).astype(F32)
    rest = stats - high
    middle = rest.astype(BF16).astype(F32)
    low = (rest - middle).astype(BF16).astype(F32)
    packed = high + pltpu.roll(middle, 16, 1) + pltpu.roll(low, 32, 1)
    return packed.astype(BF16)


def joined_stats(packed):
    packed = packed.astype(F32)
    return packed + pltpu.roll(packed, 112, 1) + pltpu.roll(packed, 96, 1)


def queries_kernel(perm, mine, other, out):
    given = stacked([unfolded(state, out.shape[1]) for state in (mine, other)])
    out[...] = jnp.dot(perm[...], given, preferred_element_type=F32).astype(BF16)


def attention_kernel(
    heads, first_row, extras,
    picked, allowed, k0, k1, k2, k3, v0, v1, v2, v3, extra, *outs,
):
    rows = picked.shape[0] // 2
    half = slice(first_row, first_row + rows)
    message = len(outs) == 1
    queries = picked[half, :]
    wide = heads * GROUP * HD
    scaling = HD ** (-0.5)
    cached = k0.shape[0]
    stack = GROUP if rows * GROUP <= 128 else 1
    permit = jnp.concatenate([allowed[half, :]] * stack, axis=0) > 0.0
    nt = (((1,), (1,)), ((), ()))
    lane = iota((rows, HD), 1)
    stats = jnp.zeros((rows, HD), F32)

    def blocks_of(refs, g, first):
        columns = slice(g * HD, (g + 1) * HD)
        parts = [ref[0:cached, columns] for ref in refs]
        rest = [extra[first : first + extras, columns]]
        at = cached + first
        rest += [ref[at : at + extras, columns] for ref in (v1, v2, v3)]
        parts.append(jnp.concatenate(rest, axis=0))
        return parts

    def scores_of(head):
        q = jnp.concatenate(
            [queries[:, (head + i) * HD : (head + i + 1) * HD] for i in range(stack)], axis=0
        )
        scores = [
            lax.dot_general(q, key, nt, preferred_element_type=F32) * scaling
            for key in blocks_of((k0, k1, k2, k3), head // GROUP, 0)
        ]
        scores[-1] = jnp.where(permit, scores[-1], NEG)
        return scores

    def weights_of(scores):
        top = functools.reduce(jnp.maximum, scores[:-1]).max(axis=1, keepdims=True)
        top = jnp.maximum(top, scores[-1].max(axis=1, keepdims=True))
        weights = [jnp.exp(s - top) for s in scores]
        total = functools.reduce(jnp.add, weights[:-1]).sum(axis=1, keepdims=True)
        return top, total + weights[-1].sum(axis=1, keepdims=True), weights

    steps = range(0, heads * GROUP, stack)
    for first in range(0, len(steps), 4):
        group = steps[first : first + 4]
        scored = [scores_of(head) for head in group]
        weighed = [weights_of(scores) for scores in scored]
        for head, (top, total, weights) in zip(group, weighed):
            values = blocks_of((v0, v1, v2, v3), head // GROUP, extras)
            weights = [w.astype(BF16) for w in weights]
            out = jnp.dot(
                jnp.concatenate(weights[:-1], axis=1),
                jnp.concatenate(values[:-1], axis=0),
                preferred_element_type=F32,
            ) + jnp.dot(weights[-1], values[-1], preferred_element_type=F32)
            out = out / total
            level = top + jnp.log(total)
            for i in range(stack):
                at = i * rows
                columns = slice((head + i) * HD, (head + i + 1) * HD)
                outs[0][:, columns] = out[at : at + rows].astype(outs[0].dtype)
                stats = jnp.where(lane == head + i, level[at : at + rows], stats)
    if message:
        outs[0][:, wide:] = split_stats(stats)
    else:
        outs[1][...] = stats


def merge(heads, kept, kept_stats, got, first, rows):
    wide = heads * GROUP * HD
    half = slice(first, first + rows)
    mine = kept_stats[half, :]
    theirs = joined_stats(got[half, wide:])
    top = jnp.maximum(mine, theirs)
    a = jnp.exp(mine - top)
    b = jnp.exp(theirs - top)
    total = a + b
    a = a / total
    b = b / total
    merged = []
    for h in range(heads * GROUP):
        columns = slice(h * HD, (h + 1) * HD)
        merged.append(
            kept[half, columns] * a[:, h : h + 1]
            + got[half, columns].astype(F32) * b[:, h : h + 1]
        )
    return merged, top + jnp.log(total)


def merge_kernel(heads, first, kept, kept_stats, got, *outs):
    wide = heads * GROUP * HD
    merged, stats = merge(heads, kept, kept_stats, got, first, kept.shape[0] // 2)
    for h, value in enumerate(merged):
        outs[0][:, h * HD : (h + 1) * HD] = value.astype(outs[0].dtype)
    if len(outs) == 1:
        outs[0][:, wide:] = split_stats(stats)
    else:
        outs[1][...] = stats


def last_kernel(heads, kept, kept_stats, got, out, squares):
    merged, _ = merge(heads, kept, kept_stats, got, 0, kept.shape[0])
    total = jnp.zeros_like(merged[0])
    for h, value in enumerate(merged):
        out[:, h * HD : (h + 1) * HD] = value
        total = total + value * value
    squares[...] = jnp.broadcast_to(total.sum(axis=1, keepdims=True), squares.shape)


def out_kernel(counts, columns_all, att, squares, other, gain, *outs):
    mean_sq = (squares[...] + other[...])[:, 0:1] / columns_all
    normed = att[...] * lax.rsqrt(mean_sq + EPS) * gain[...]
    at = 0
    for count, out in zip(counts, outs):
        out[...] = normed[at : at + count].astype(BF16)
        at += count


def per_device(
    cache_k,
    cache_v,
    span_q,
    span_k,
    span_v,
    span_frames,
    action_ids,
    action_table,
    frame_q,
    frame_k,
    frame_v,
    revealed_k,
    revealed_v,
    mask_k,
    mask_v,
    pass1_idx,
    pass2_idx,
    out_gain,
):
    owners = lax.axis_size("ctx")
    tp = lax.axis_size("tp")
    me = lax.axis_index("ctx")
    blocks = owners // 4
    spans = span_k.shape[0]
    frames = frame_k.shape[0]
    width = span_k.shape[1]
    q_width = span_q.shape[1]
    heads = width // HD
    n1 = pass1_idx.shape[0] // owners
    n2 = pass2_idx.shape[0] // owners
    picked = n1 + n2
    block_rows = -(-(spans + picked) // 8) * 8
    rows = blocks * block_rows

    bits = [(1 << b) + 1 for b in range(2, owners.bit_length() - 1)][::-1]

    depth = (blocks // 2) * spans + blocks * picked
    extras = 3 * spans

    q3 = exchange(frame_q, "ctx", 3)
    small = (
        action_ids[None, :], pass1_idx[None, :], pass2_idx[None, :],
        action_table, span_k, span_v, frame_k, frame_v, revealed_k, revealed_v,
        mask_k, mask_v,
    )
    place = me.reshape(1)
    values, extra, token = call(
        functools.partial(keys_kernel, (spans, frames)),
        "plane_values",
        [
            jax.ShapeDtypeStruct((cache_v.shape[0] + 2 * extras, width), BF16),
            jax.ShapeDtypeStruct((2 * extras, width), BF16),
            jax.ShapeDtypeStruct((8, HD), F32),
        ],
        place, *small, cache_v,
        places={0: pltpu.SMEM, **{i + 1: pl.ANY for i in range(len(small) + 1)}},
        scratch=[pltpu.VMEM(array.shape, array.dtype) for array in small]
        + [pltpu.SemaphoreType.DMA((len(small) + 1,))],
        limit=PLAN_LIMIT,
        cost=pl.CostEstimate(flops=PLAN_FLOPS, bytes_accessed=PLAN_BYTES, transcendentals=0),
    )
    k0, chip, own_spans = call(
        stage_kernel,
        "queries_arrived",
        [
            jax.ShapeDtypeStruct(cache_k.shape, BF16),
            jax.ShapeDtypeStruct((2 * frames, q_width), BF16),
            jax.ShapeDtypeStruct(span_q.shape, BF16),
        ],
        cache_k, span_q, frame_q, q3,
    )
    other_chip = exchange(chip, "ctx", 1)
    idx1, idx2 = call(
        listed_kernel,
        "listed",
        [jax.ShapeDtypeStruct((1, idx.shape[0]), idx.dtype) for idx in (pass1_idx, pass2_idx)],
        token, pass1_idx[None, :], pass2_idx[None, :],
        places={0: pl.ANY},
        cost=pl.CostEstimate(flops=PLAN_FLOPS, bytes_accessed=PLAN_BYTES, transcendentals=0),
    )
    k3 = exchange(cache_k, "ctx", 3)
    v3 = exchange(values, "ctx", 3)
    k1 = exchange(k0, "ctx", 1)
    v1 = exchange(values, "ctx", 1)

    state = call(
        functools.partial(select_kernel, (spans, frames, n1, n2, len(bits))),
        "column_queries",
        jax.ShapeDtypeStruct((spans + blocks * picked, q_width), BF16),
        place, idx1, idx2, own_spans, chip, other_chip,
        places={0: pltpu.SMEM},
    )

    held = spans
    for bit in bits[:-1]:
        fold = 2 if bit == bits[-2] and (state.shape[0] + held) % 8 else 1
        other = exchange(state, "ctx", bit)
        state, k3, k1 = call(
            functools.partial(grow_kernel, held),
            "more_queries",
            [
                jax.ShapeDtypeStruct(
                    (fold * (state.shape[0] + held), q_width // fold), BF16
                ),
                jax.ShapeDtypeStruct(k3.shape, BF16),
                jax.ShapeDtypeStruct(k1.shape, BF16),
            ],
            state, other, k3, k1,
            places={2: pl.ANY, 3: pl.ANY},
            aliases={2: 1, 3: 2},
        )
        held = 2 * held
    other = exchange(state, "ctx", bits[-1])
    k2 = exchange(k3, "ctx", 1)
    other, v3, k2 = tie(other, v3, k2)
    v2 = exchange(v3, "ctx", 1)

    perm, allowed = call(
        functools.partial(plan_kernel, (spans, n1, n2, blocks, block_rows, len(bits), extras)),
        "row_plan",
        [
            jax.ShapeDtypeStruct((rows, 2 * depth), BF16),
            jax.ShapeDtypeStruct((rows, 4 * extras), F32),
        ],
        place, span_frames[None, :],
        places={0: pltpu.SMEM},
    )
    keep = rows // 2
    packed = q_width + HD
    queries = call(
        queries_kernel,
        "ordered_queries",
        jax.ShapeDtypeStruct((rows, q_width), BF16),
        perm, state, other,
    )
    given = (queries, allowed, k0, k1, k2, k3, cache_v, v1, v2, v3, extra)
    limit = (16 if blocks <= 4 else 40) * 2**20
    send = call(
        functools.partial(attention_kernel, heads, keep, extras),
        "sent_attention",
        jax.ShapeDtypeStruct((keep, packed), BF16),
        *given,
        limit=limit,
    )
    kept, stats = call(
        functools.partial(attention_kernel, heads, 0, extras),
        "kept_attention",
        [
            jax.ShapeDtypeStruct((keep, q_width), F32),
            jax.ShapeDtypeStruct((keep, HD), F32),
        ],
        *given,
        limit=limit,
    )
    for bit in bits[:0:-1]:
        got = exchange(send, "ctx", bit)
        keep = keep // 2
        given = (kept, stats, got)
        send = call(
            functools.partial(merge_kernel, heads, keep),
            "sent_partials",
            jax.ShapeDtypeStruct((keep, packed), BF16),
            *given,
        )
        kept, stats = call(
            functools.partial(merge_kernel, heads, 0),
            "kept_partials",
            [
                jax.ShapeDtypeStruct((keep, q_width), F32),
                jax.ShapeDtypeStruct((keep, HD), F32),
            ],
            *given,
        )
    got = exchange(send, "ctx", bits[0])
    att, squares = call(
        functools.partial(last_kernel, heads),
        "merge_last",
        [
            jax.ShapeDtypeStruct((block_rows, q_width), F32),
            jax.ShapeDtypeStruct((block_rows, HD), F32),
        ],
        kept, stats, got,
    )
    other_squares = exchange(squares, "tp", 1)
    counts = (spans, n1, n2)
    return tuple(
        call(
            functools.partial(out_kernel, counts, float(tp * q_width)),
            "normalize",
            [jax.ShapeDtypeStruct((count, q_width), BF16) for count in counts],
            att, squares, other_squares, out_gain[None, :],
        )
    )


def solution(mesh):
    in_specs = (
        P("ctx", "tp"),
        P("ctx", "tp"),
        P("ctx", "tp"),
        P("ctx", "tp"),
        P("ctx", "tp"),
        P(),
        P("ctx"),
        P(None, "tp"),
        P("ctx", "tp"),
        P("ctx", "tp"),
        P("ctx", "tp"),
        P("ctx", "tp"),
        P("ctx", "tp"),
        P("tp"),
        P("tp"),
        P(),
        P(),
        P("tp"),
    )
    out_specs = (P("ctx", "tp"), P("ctx", "tp"), P("ctx", "tp"))
    return jax.shard_map(
        per_device, mesh=mesh, in_specs=in_specs, out_specs=out_specs, check_vma=False
    )
```

```python
import functools

import jax
import jax.numpy as jnp
from jax import lax
from jax.experimental import pallas as pl
from jax.experimental.pallas import tpu as pltpu
from jax.sharding import PartitionSpec as P

HD = 128
GROUP = 4
NEG = -1e30
EPS = 1e-6
F32 = jnp.float32
BF16 = jnp.bfloat16
VMEM = pltpu.VMEM
PLAN_LIMIT = 59 * 2**20
PLAN_BYTES = 108000000
PLAN_FLOPS = 34500000000


def exchange(value, axis, mask):
    pairs = [(source, source ^ mask) for source in range(lax.axis_size(axis))]
    return lax.ppermute(value, axis, pairs)


def call(
    kernel, name, out_shape, *operands, scratch=(), places=None, cost=None, aliases=None, out_any=(), limit=16 * 2**20
):
    places = places or {}
    in_specs = [
        pl.BlockSpec(memory_space=places.get(i, VMEM)) for i in range(len(operands))
    ]
    single = not isinstance(out_shape, (list, tuple))
    out_specs = pl.BlockSpec(memory_space=VMEM)
    aliases = aliases or {}
    if not single:
        moved = {*aliases.values(), *out_any}
        out_specs = [
            pl.BlockSpec(memory_space=pl.ANY if i in moved else VMEM)
            for i in range(len(out_shape))
        ]
    return pl.pallas_call(
        kernel,
        out_shape=out_shape,
        in_specs=in_specs,
        out_specs=out_specs,
        scratch_shapes=list(scratch),
        input_output_aliases=aliases,
        compiler_params=pltpu.CompilerParams(vmem_limit_bytes=limit),
        cost_estimate=cost,
        name=name,
    )(*operands)


def iota(shape, dim):
    return lax.broadcasted_iota(jnp.int32, shape, dim)


def split_index(index, size):
    whole = ((index.astype(F32) + 0.5) * (1.0 / size)).astype(jnp.int32)
    return whole, index - whole * size


def at_lane(row, index):
    lanes = iota((index.shape[0], row.shape[1]), 1)
    return jnp.where(lanes == index, row.astype(F32), 0.0).sum(axis=1, keepdims=True)


def parity(index, count):
    total = jnp.zeros_like(index)
    for i in range(count):
        total = total ^ (index >> i)
    return total & 1


def fetch(given, held, sems):
    copies = [
        pltpu.make_async_copy(source, target, sems.at[i])
        for i, (source, target) in enumerate(zip(given, held))
    ]
    for copy in copies:
        copy.start()
    return copies


def keys_kernel(
    sizes, place,
    ids_h, idx1_h, idx2_h, table_h, span_k_h, span_v_h,
    fk_h, fv_h, rk_h, rv_h, mk_h, mv_h, cache_v_h,
    values, extra, done, *scratch,
):
    spans, frames = sizes
    given = (ids_h, idx1_h, idx2_h, table_h, span_k_h, span_v_h,
             fk_h, fv_h, rk_h, rv_h, mk_h, mv_h, cache_v_h)
    held, sems = scratch[:-1], scratch[-1]
    cached = cache_v_h.shape[0]
    copies = fetch(given, (*held, values.at[0:cached]), sems)
    for copy in copies[:-1]:
        copy.wait()
    ids, idx1, idx2, table, span_k, span_v, fk, fv, rk, rv, mk, mv = held
    me = place[0]

    hits = at_lane(ids[...], iota((spans, 1), 0))
    hits = (iota((spans, table.shape[0]), 1).astype(F32) == hits).astype(BF16)
    terms = jnp.dot(hits, table[...], preferred_element_type=F32)
    position = me * frames + iota((frames, 1), 0)

    def listed(idx):
        same = jnp.where(idx[...] == position, 1.0, 0.0)
        return same.sum(axis=1, keepdims=True) > 0.0

    first = listed(idx1)
    second = listed(idx2)
    sets = [span_k[...].astype(F32) + terms, span_v[...].astype(F32)]
    shown = []
    for frame, revealed, token in ((fk, rk, mk), (fv, rv, mv)):
        frame = frame[...].astype(F32)
        token = token[...].astype(F32).reshape(1, -1)
        sets.append(jnp.where(first, token, frame))
        shown.append(
            jnp.where(second, token, jnp.where(first, revealed[...].astype(F32), frame))
        )
    sets += shown
    half = extra.shape[0] // 2
    rest = jnp.zeros((half - 3 * spans, extra.shape[1]), F32)
    parts = jnp.concatenate([*sets[0::2], rest, *sets[1::2], rest], axis=0).astype(BF16)
    extra[...] = parts
    values[cached:, :] = parts
    done[...] = jnp.zeros(done.shape, F32)
    copies[-1].wait()


def plan_kernel(sizes, place, span_frames, perm, allowed):
    spans, n1, n2, blocks, block_rows, mask_bits, extras = sizes
    me = place[0]
    own_block = me >> 2
    picked = n1 + n2

    rows, both = perm.shape
    depth = both // 2
    row = iota((rows, 1), 0)
    block, at = split_index(row, block_rows)
    mask = parity(block, mask_bits)
    for i in range(mask_bits):
        mask = mask + (((block >> i) & 1) << (mask_bits + 1 - i))
    half = blocks // 2
    span_at = block * spans + at + jnp.where(block < half, 0, depth - half * spans)
    pick_at = depth - blocks * picked + (own_block ^ (mask >> 2)) * picked + at - spans
    is_span = at < spans
    is_pick = (at >= spans) & (at < spans + picked)
    lane = iota((1, both), 1)
    same = (is_span & (lane == span_at)) | (
        is_pick & ((lane == pick_at) | (lane == pick_at + depth))
    )
    perm[...] = jnp.where(same, 1.0, 0.0).astype(BF16)

    count = allowed.shape[1]
    lane = iota((1, count), 1)
    member, key_at = split_index(lane, extras)
    key = jnp.where(key_at < spans, (member ^ me) * spans + key_at, -1)
    total = span_frames.shape[1]
    numbers = jnp.broadcast_to(span_frames[...].astype(F32), (8, total)).astype(BF16)
    key_hits = jnp.where(iota((total, 1), 0) == key, 1.0, 0.0).astype(BF16)
    key_frames = jnp.dot(numbers, key_hits, preferred_element_type=F32)[0:1]
    row_frames = at_lane(span_frames[...], jnp.where(is_span, (me ^ mask) * spans + at, -1))
    sees = (key_at < spans) & ((at >= spans) | (key_frames <= row_frames))
    in_first = (key_at >= spans) & (key_at < 2 * spans)
    in_second = (key_at >= 2 * spans) & (key_at < 3 * spans)
    sees = sees | (in_first & is_pick & (at < spans + n1))
    sees = sees | (in_second & is_pick & (at >= spans + n1))
    allowed[...] = jnp.where(sees, 1.0, 0.0)


def stacked(parts):
    return jnp.concatenate([part.astype(F32) for part in parts], axis=0).astype(BF16)


def select_kernel(sizes, place, idx1, idx2, span_q, pair, other, out):
    spans, frames, n1, n2, mask_bits = sizes
    me = place[0]
    column = (me & 3) ^ parity(me >> 2, mask_bits)
    picked = n1 + n2
    shape = (out.shape[0], spans + 4 * frames)
    row = iota((shape[0], 1), 0)
    block, at = split_index(jnp.maximum(row - spans, 0), picked)
    owner = block * 4 + (column ^ parity(block, mask_bits))
    wanted = jnp.where(
        at < n1,
        at_lane(idx1[...], owner * n1 + at),
        at_lane(idx2[...], owner * n2 + at - n1),
    )
    lane = iota((1, shape[1]), 1)
    member, at = split_index(jnp.maximum(lane - spans, 0), frames)
    position = ((member ^ me) * frames + at).astype(F32)
    chosen = jnp.where((lane >= spans) & (row >= spans) & (wanted == position), 1.0, 0.0)
    copied = jnp.where((row < spans) & (lane == row), 1.0, 0.0)
    pick = (chosen + copied).astype(BF16)
    given = stacked([span_q[...], pair[0:frames], other[...], pair[frames:]])
    out[...] = jnp.dot(pick, given, preferred_element_type=F32).astype(BF16)


def tie_kernel(*_):
    pass


def listed_kernel(_, idx1, idx2, out1, out2):
    out1[...] = idx1[...]
    out2[...] = idx2[...]


def stage_kernel(cached, spans, mine, other, copied, pair, copied_spans):
    copied[...] = cached[...]
    copied_spans[...] = spans[...]
    pair[...] = stacked([mine[...], other[...]])


def tie(*arrays):
    count = len(arrays)
    return call(
        tie_kernel,
        "arrived",
        [jax.ShapeDtypeStruct(array.shape, array.dtype) for array in arrays],
        *arrays,
        places={i: pl.ANY for i in range(count)},
        aliases={i: i for i in range(count)},
    )


def grow_kernel(spans, mine, other, _, __, out, *___):
    a = mine[...].astype(F32)
    b = other[...].astype(F32)
    parts = [a[:spans], b[:spans], a[spans:] + b[spans:]]
    width = out.shape[1]
    pieces = [p[:, at : at + width] for at in range(0, a.shape[1], width) for p in parts]
    out[...] = jnp.concatenate(pieces, axis=0).astype(BF16)


def unfolded(state, width):
    state = state[...].astype(F32)
    count = state.shape[0] * state.shape[1] // width
    return jnp.concatenate(
        [state[at : at + count] for at in range(0, state.shape[0], count)], axis=1
    )


def split_stats(stats):
    lane = lax.broadcasted_iota(jnp.int32, stats.shape, 1)
    stats = jnp.where(lane < 16, stats, 0.0)
    high = stats.astype(BF16).astype(F32)
    rest = stats - high
    middle = rest.astype(BF16).astype(F32)
    low = (rest - middle).astype(BF16).astype(F32)
    packed = high + pltpu.roll(middle, 16, 1) + pltpu.roll(low, 32, 1)
    return packed.astype(BF16)


def joined_stats(packed):
    packed = packed.astype(F32)
    return packed + pltpu.roll(packed, 112, 1) + pltpu.roll(packed, 96, 1)


def queries_kernel(perm, mine, other, out):
    given = stacked([unfolded(state, out.shape[1]) for state in (mine, other)])
    out[...] = jnp.dot(perm[...], given, preferred_element_type=F32).astype(BF16)


def attention_kernel(
    heads, first_row, extras,
    picked, allowed, k0, k1, k2, k3, v0, v1, v2, v3, extra, *outs,
):
    rows = picked.shape[0] // 2
    half = slice(first_row, first_row + rows)
    message = len(outs) == 1
    queries = picked[half, :]
    wide = heads * GROUP * HD
    scaling = HD ** (-0.5)
    cached = k0.shape[0]
    stack = GROUP if rows * GROUP <= 128 else 1
    permit = jnp.concatenate([allowed[half, :]] * stack, axis=0) > 0.0
    nt = (((1,), (1,)), ((), ()))
    lane = iota((rows, HD), 1)
    stats = jnp.zeros((rows, HD), F32)

    def blocks_of(refs, g, first):
        columns = slice(g * HD, (g + 1) * HD)
        parts = [ref[0:cached, columns] for ref in refs]
        rest = [extra[first : first + extras, columns]]
        at = cached + first
        rest += [ref[at : at + extras, columns] for ref in (v1, v2, v3)]
        parts.append(jnp.concatenate(rest, axis=0))
        return parts

    def scores_of(head):
        q = jnp.concatenate(
            [queries[:, (head + i) * HD : (head + i + 1) * HD] for i in range(stack)], axis=0
        )
        scores = [
            lax.dot_general(q, key, nt, preferred_element_type=F32) * scaling
            for key in blocks_of((k0, k1, k2, k3), head // GROUP, 0)
        ]
        scores[-1] = jnp.where(permit, scores[-1], NEG)
        return scores

    def weights_of(scores):
        top = functools.reduce(jnp.maximum, scores[:-1]).max(axis=1, keepdims=True)
        top = jnp.maximum(top, scores[-1].max(axis=1, keepdims=True))
        weights = [jnp.exp(s - top) for s in scores]
        total = functools.reduce(jnp.add, weights[:-1]).sum(axis=1, keepdims=True)
        return top, total + weights[-1].sum(axis=1, keepdims=True), weights

    steps = range(0, heads * GROUP, stack)
    for first in range(0, len(steps), 4):
        group = steps[first : first + 4]
        scored = [scores_of(head) for head in group]
        weighed = [weights_of(scores) for scores in scored]
        for head, (top, total, weights) in zip(group, weighed):
            values = blocks_of((v0, v1, v2, v3), head // GROUP, extras)
            weights = [w.astype(BF16) for w in weights]
            out = jnp.dot(
                jnp.concatenate(weights[:-1], axis=1),
                jnp.concatenate(values[:-1], axis=0),
                preferred_element_type=F32,
            ) + jnp.dot(weights[-1], values[-1], preferred_element_type=F32)
            out = out / total
            level = top + jnp.log(total)
            for i in range(stack):
                at = i * rows
                columns = slice((head + i) * HD, (head + i + 1) * HD)
                outs[0][:, columns] = out[at : at + rows].astype(outs[0].dtype)
                stats = jnp.where(lane == head + i, level[at : at + rows], stats)
    if message:
        outs[0][:, wide:] = split_stats(stats)
    else:
        outs[1][...] = stats


def merge(heads, kept, kept_stats, got, first, rows):
    wide = heads * GROUP * HD
    half = slice(first, first + rows)
    mine = kept_stats[half, :]
    theirs = joined_stats(got[half, wide:])
    top = jnp.maximum(mine, theirs)
    a = jnp.exp(mine - top)
    b = jnp.exp(theirs - top)
    total = a + b
    a = a / total
    b = b / total
    merged = []
    for h in range(heads * GROUP):
        columns = slice(h * HD, (h + 1) * HD)
        merged.append(
            kept[half, columns] * a[:, h : h + 1]
            + got[half, columns].astype(F32) * b[:, h : h + 1]
        )
    return merged, top + jnp.log(total)


def merge_kernel(heads, first, kept, kept_stats, got, *outs):
    wide = heads * GROUP * HD
    merged, stats = merge(heads, kept, kept_stats, got, first, kept.shape[0] // 2)
    for h, value in enumerate(merged):
        outs[0][:, h * HD : (h + 1) * HD] = value.astype(outs[0].dtype)
    if len(outs) == 1:
        outs[0][:, wide:] = split_stats(stats)
    else:
        outs[1][...] = stats


def last_kernel(heads, kept, kept_stats, got, out, squares):
    merged, _ = merge(heads, kept, kept_stats, got, 0, kept.shape[0])
    total = jnp.zeros_like(merged[0])
    for h, value in enumerate(merged):
        out[:, h * HD : (h + 1) * HD] = value
        total = total + value * value
    squares[...] = jnp.broadcast_to(total.sum(axis=1, keepdims=True), squares.shape)


def out_kernel(counts, columns_all, att, squares, other, gain, *outs):
    mean_sq = (squares[...] + other[...])[:, 0:1] / columns_all
    normed = att[...] * lax.rsqrt(mean_sq + EPS) * gain[...]
    at = 0
    for count, out in zip(counts, outs):
        out[...] = normed[at : at + count].astype(BF16)
        at += count


def per_device(
    cache_k,
    cache_v,
    span_q,
    span_k,
    span_v,
    span_frames,
    action_ids,
    action_table,
    frame_q,
    frame_k,
    frame_v,
    revealed_k,
    revealed_v,
    mask_k,
    mask_v,
    pass1_idx,
    pass2_idx,
    out_gain,
):
    owners = lax.axis_size("ctx")
    tp = lax.axis_size("tp")
    me = lax.axis_index("ctx")
    blocks = owners // 4
    spans = span_k.shape[0]
    frames = frame_k.shape[0]
    width = span_k.shape[1]
    q_width = span_q.shape[1]
    heads = width // HD
    n1 = pass1_idx.shape[0] // owners
    n2 = pass2_idx.shape[0] // owners
    picked = n1 + n2
    block_rows = -(-(spans + picked) // 8) * 8
    rows = blocks * block_rows

    bits = [(1 << b) + 1 for b in range(2, owners.bit_length() - 1)][::-1]

    depth = (blocks // 2) * spans + blocks * picked
    extras = -(-3 * spans // 16) * 16

    q3 = exchange(frame_q, "ctx", 3)
    small = (
        action_ids[None, :], pass1_idx[None, :], pass2_idx[None, :],
        action_table, span_k, span_v, frame_k, frame_v, revealed_k, revealed_v,
        mask_k, mask_v,
    )
    place = me.reshape(1)
    values, extra, token = call(
        functools.partial(keys_kernel, (spans, frames)),
        "plane_values",
        [
            jax.ShapeDtypeStruct((cache_v.shape[0] + 2 * extras, width), BF16),
            jax.ShapeDtypeStruct((2 * extras, width), BF16),
            jax.ShapeDtypeStruct((8, HD), F32),
        ],
        place, *small, cache_v,
        places={0: pltpu.SMEM, **{i + 1: pl.ANY for i in range(len(small) + 1)}},
        scratch=[pltpu.VMEM(array.shape, array.dtype) for array in small]
        + [pltpu.SemaphoreType.DMA((len(small) + 1,))],
        limit=PLAN_LIMIT,
        cost=pl.CostEstimate(flops=PLAN_FLOPS, bytes_accessed=PLAN_BYTES, transcendentals=0),
    )
    k0, chip, own_spans = call(
        stage_kernel,
        "queries_arrived",
        [
            jax.ShapeDtypeStruct(cache_k.shape, BF16),
            jax.ShapeDtypeStruct((2 * frames, q_width), BF16),
            jax.ShapeDtypeStruct(span_q.shape, BF16),
        ],
        cache_k, span_q, frame_q, q3,
    )
    other_chip = exchange(chip, "ctx", 1)
    idx1, idx2 = call(
        listed_kernel,
        "listed",
        [jax.ShapeDtypeStruct((1, idx.shape[0]), idx.dtype) for idx in (pass1_idx, pass2_idx)],
        token, pass1_idx[None, :], pass2_idx[None, :],
        places={0: pl.ANY},
        cost=pl.CostEstimate(flops=PLAN_FLOPS, bytes_accessed=PLAN_BYTES, transcendentals=0),
    )
    k3 = exchange(cache_k, "ctx", 3)
    v3 = exchange(values, "ctx", 3)
    k1 = exchange(k0, "ctx", 1)
    v1 = exchange(values, "ctx", 1)

    state = call(
        functools.partial(select_kernel, (spans, frames, n1, n2, len(bits))),
        "column_queries",
        jax.ShapeDtypeStruct((spans + blocks * picked, q_width), BF16),
        place, idx1, idx2, own_spans, chip, other_chip,
        places={0: pltpu.SMEM},
    )

    held = spans
    for bit in bits[:-1]:
        fold = 2 if bit == bits[-2] and (state.shape[0] + held) % 8 else 1
        other = exchange(state, "ctx", bit)
        state, k3, k1 = call(
            functools.partial(grow_kernel, held),
            "more_queries",
            [
                jax.ShapeDtypeStruct(
                    (fold * (state.shape[0] + held), q_width // fold), BF16
                ),
                jax.ShapeDtypeStruct(k3.shape, BF16),
                jax.ShapeDtypeStruct(k1.shape, BF16),
            ],
            state, other, k3, k1,
            places={2: pl.ANY, 3: pl.ANY},
            aliases={2: 1, 3: 2},
        )
        held = 2 * held
    other = exchange(state, "ctx", bits[-1])
    k2 = exchange(k3, "ctx", 1)
    other, v3, k2 = tie(other, v3, k2)
    v2 = exchange(v3, "ctx", 1)

    perm, allowed = call(
        functools.partial(plan_kernel, (spans, n1, n2, blocks, block_rows, len(bits), extras)),
        "row_plan",
        [
            jax.ShapeDtypeStruct((rows, 2 * depth), BF16),
            jax.ShapeDtypeStruct((rows, 4 * extras), F32),
        ],
        place, span_frames[None, :],
        places={0: pltpu.SMEM},
    )
    keep = rows // 2
    packed = q_width + HD
    queries = call(
        queries_kernel,
        "ordered_queries",
        jax.ShapeDtypeStruct((rows, q_width), BF16),
        perm, state, other,
    )
    given = (queries, allowed, k0, k1, k2, k3, cache_v, v1, v2, v3, extra)
    limit = (16 if blocks <= 4 else 40) * 2**20
    send = call(
        functools.partial(attention_kernel, heads, keep, extras),
        "sent_attention",
        jax.ShapeDtypeStruct((keep, packed), BF16),
        *given,
        limit=limit,
    )
    kept, stats = call(
        functools.partial(attention_kernel, heads, 0, extras),
        "kept_attention",
        [
            jax.ShapeDtypeStruct((keep, q_width), F32),
            jax.ShapeDtypeStruct((keep, HD), F32),
        ],
        *given,
        limit=limit,
    )
    for bit in bits[:0:-1]:
        got = exchange(send, "ctx", bit)
        keep = keep // 2
        given = (kept, stats, got)
        send = call(
            functools.partial(merge_kernel, heads, keep),
            "sent_partials",
            jax.ShapeDtypeStruct((keep, packed), BF16),
            *given,
        )
        kept, stats = call(
            functools.partial(merge_kernel, heads, 0),
            "kept_partials",
            [
                jax.ShapeDtypeStruct((keep, q_width), F32),
                jax.ShapeDtypeStruct((keep, HD), F32),
            ],
            *given,
        )
    got = exchange(send, "ctx", bits[0])
    att, squares = call(
        functools.partial(last_kernel, heads),
        "merge_last",
        [
            jax.ShapeDtypeStruct((block_rows, q_width), F32),
            jax.ShapeDtypeStruct((block_rows, HD), F32),
        ],
        kept, stats, got,
    )
    other_squares = exchange(squares, "tp", 1)
    counts = (spans, n1, n2)
    return tuple(
        call(
            functools.partial(out_kernel, counts, float(tp * q_width)),
            "normalize",
            [jax.ShapeDtypeStruct((count, q_width), BF16) for count in counts],
            att, squares, other_squares, out_gain[None, :],
        )
    )


def solution(mesh):
    in_specs = (
        P("ctx", "tp"),
        P("ctx", "tp"),
        P("ctx", "tp"),
        P("ctx", "tp"),
        P("ctx", "tp"),
        P(),
        P("ctx"),
        P(None, "tp"),
        P("ctx", "tp"),
        P("ctx", "tp"),
        P("ctx", "tp"),
        P("ctx", "tp"),
        P("ctx", "tp"),
        P("tp"),
        P("tp"),
        P(),
        P(),
        P("tp"),
    )
    out_specs = (P("ctx", "tp"), P("ctx", "tp"), P("ctx", "tp"))
    return jax.shard_map(
        per_device, mesh=mesh, in_specs=in_specs, out_specs=out_specs, check_vma=False
    )
```

```python
import functools

import jax
import jax.numpy as jnp
from jax import lax
from jax.experimental import pallas as pl
from jax.experimental.pallas import tpu as pltpu
from jax.sharding import PartitionSpec as P

HD = 128
GROUP = 4
NEG = -1e30
EPS = 1e-6
F32 = jnp.float32
BF16 = jnp.bfloat16
VMEM = pltpu.VMEM
PLAN_LIMIT = 59 * 2**20
PLAN_BYTES = 108000000
PLAN_FLOPS = 34500000000


def exchange(value, axis, mask):
    pairs = [(source, source ^ mask) for source in range(lax.axis_size(axis))]
    return lax.ppermute(value, axis, pairs)


def call(
    kernel, name, out_shape, *operands, scratch=(), places=None, cost=None, aliases=None, out_any=(), limit=16 * 2**20
):
    places = places or {}
    in_specs = [
        pl.BlockSpec(memory_space=places.get(i, VMEM)) for i in range(len(operands))
    ]
    single = not isinstance(out_shape, (list, tuple))
    out_specs = pl.BlockSpec(memory_space=VMEM)
    aliases = aliases or {}
    if not single:
        moved = {*aliases.values(), *out_any}
        out_specs = [
            pl.BlockSpec(memory_space=pl.ANY if i in moved else VMEM)
            for i in range(len(out_shape))
        ]
    return pl.pallas_call(
        kernel,
        out_shape=out_shape,
        in_specs=in_specs,
        out_specs=out_specs,
        scratch_shapes=list(scratch),
        input_output_aliases=aliases,
        compiler_params=pltpu.CompilerParams(vmem_limit_bytes=limit),
        cost_estimate=cost,
        name=name,
    )(*operands)


def iota(shape, dim):
    return lax.broadcasted_iota(jnp.int32, shape, dim)


def split_index(index, size):
    whole = ((index.astype(F32) + 0.5) * (1.0 / size)).astype(jnp.int32)
    return whole, index - whole * size


def at_lane(row, index):
    lanes = iota((index.shape[0], row.shape[1]), 1)
    return jnp.where(lanes == index, row.astype(F32), 0.0).sum(axis=1, keepdims=True)


def parity(index, count):
    total = jnp.zeros_like(index)
    for i in range(count):
        total = total ^ (index >> i)
    return total & 1


def fetch(given, held, sems):
    copies = [
        pltpu.make_async_copy(source, target, sems.at[i])
        for i, (source, target) in enumerate(zip(given, held))
    ]
    for copy in copies:
        copy.start()
    return copies


def keys_kernel(
    sizes, place,
    ids_h, idx1_h, idx2_h, table_h, span_k_h, span_v_h,
    fk_h, fv_h, rk_h, rv_h, mk_h, mv_h, cache_v_h,
    values, extra, done, *scratch,
):
    spans, frames = sizes
    given = (ids_h, idx1_h, idx2_h, table_h, span_k_h, span_v_h,
             fk_h, fv_h, rk_h, rv_h, mk_h, mv_h, cache_v_h)
    held, sems = scratch[:-1], scratch[-1]
    cached = cache_v_h.shape[0]
    copies = fetch(given, (*held, values.at[0:cached]), sems)
    for copy in copies[:-1]:
        copy.wait()
    ids, idx1, idx2, table, span_k, span_v, fk, fv, rk, rv, mk, mv = held
    me = place[0]

    hits = at_lane(ids[...], iota((spans, 1), 0))
    hits = (iota((spans, table.shape[0]), 1).astype(F32) == hits).astype(BF16)
    terms = jnp.dot(hits, table[...], preferred_element_type=F32)
    position = me * frames + iota((frames, 1), 0)

    def listed(idx):
        same = jnp.where(idx[...] == position, 1.0, 0.0)
        return same.sum(axis=1, keepdims=True) > 0.0

    first = listed(idx1)
    second = listed(idx2)
    sets = [span_k[...].astype(F32) + terms, span_v[...].astype(F32)]
    shown = []
    for frame, revealed, token in ((fk, rk, mk), (fv, rv, mv)):
        frame = frame[...].astype(F32)
        token = token[...].astype(F32).reshape(1, -1)
        sets.append(jnp.where(first, token, frame))
        shown.append(
            jnp.where(second, token, jnp.where(first, revealed[...].astype(F32), frame))
        )
    sets += shown
    half = extra.shape[0] // 2
    rest = jnp.zeros((half - 3 * spans, extra.shape[1]), F32)
    parts = jnp.concatenate([*sets[0::2], rest, *sets[1::2], rest], axis=0).astype(BF16)
    extra[...] = parts
    values[cached:, :] = parts
    done[...] = jnp.zeros(done.shape, F32)
    copies[-1].wait()


def plan_kernel(sizes, place, span_frames, perm, allowed):
    spans, n1, n2, blocks, block_rows, mask_bits, extras = sizes
    me = place[0]
    own_block = me >> 2
    picked = n1 + n2

    rows, both = perm.shape
    depth = both // 2
    row = iota((rows, 1), 0)
    block, at = split_index(row, block_rows)
    mask = parity(block, mask_bits)
    for i in range(mask_bits):
        mask = mask + (((block >> i) & 1) << (mask_bits + 1 - i))
    half = blocks // 2
    span_at = block * spans + at + jnp.where(block < half, 0, depth - half * spans)
    pick_at = depth - blocks * picked + (own_block ^ (mask >> 2)) * picked + at - spans
    is_span = at < spans
    is_pick = (at >= spans) & (at < spans + picked)
    lane = iota((1, both), 1)
    same = (is_span & (lane == span_at)) | (
        is_pick & ((lane == pick_at) | (lane == pick_at + depth))
    )
    perm[...] = jnp.where(same, 1.0, 0.0).astype(BF16)

    count = allowed.shape[1]
    lane = iota((1, count), 1)
    member, key_at = split_index(lane, extras)
    key = jnp.where(key_at < spans, (member ^ me) * spans + key_at, -1)
    total = span_frames.shape[1]
    numbers = jnp.broadcast_to(span_frames[...].astype(F32), (8, total)).astype(BF16)
    key_hits = jnp.where(iota((total, 1), 0) == key, 1.0, 0.0).astype(BF16)
    key_frames = jnp.dot(numbers, key_hits, preferred_element_type=F32)[0:1]
    row_frames = at_lane(span_frames[...], jnp.where(is_span, (me ^ mask) * spans + at, -1))
    sees = (key_at < spans) & ((at >= spans) | (key_frames <= row_frames))
    in_first = (key_at >= spans) & (key_at < 2 * spans)
    in_second = (key_at >= 2 * spans) & (key_at < 3 * spans)
    sees = sees | (in_first & is_pick & (at < spans + n1))
    sees = sees | (in_second & is_pick & (at >= spans + n1))
    allowed[...] = jnp.where(sees, 1.0, 0.0)


def stacked(parts):
    return jnp.concatenate([part.astype(F32) for part in parts], axis=0).astype(BF16)


def select_kernel(sizes, place, idx1, idx2, span_q, pair, other, out):
    spans, frames, n1, n2, mask_bits = sizes
    me = place[0]
    column = (me & 3) ^ parity(me >> 2, mask_bits)
    picked = n1 + n2
    shape = (out.shape[0], spans + 4 * frames)
    row = iota((shape[0], 1), 0)
    block, at = split_index(jnp.maximum(row - spans, 0), picked)
    owner = block * 4 + (column ^ parity(block, mask_bits))
    wanted = jnp.where(
        at < n1,
        at_lane(idx1[...], owner * n1 + at),
        at_lane(idx2[...], owner * n2 + at - n1),
    )
    lane = iota((1, shape[1]), 1)
    member, at = split_index(jnp.maximum(lane - spans, 0), frames)
    position = ((member ^ me) * frames + at).astype(F32)
    chosen = jnp.where((lane >= spans) & (row >= spans) & (wanted == position), 1.0, 0.0)
    copied = jnp.where((row < spans) & (lane == row), 1.0, 0.0)
    pick = (chosen + copied).astype(BF16)
    given = stacked([span_q[...], pair[0:frames], other[...], pair[frames:]])
    out[...] = jnp.dot(pick, given, preferred_element_type=F32).astype(BF16)


def tie_kernel(*_):
    pass


def listed_kernel(_, idx1, idx2, out1, out2):
    out1[...] = idx1[...]
    out2[...] = idx2[...]


def stage_kernel(cached, spans, mine, other, copied, pair, copied_spans):
    copied[...] = cached[...]
    copied_spans[...] = spans[...]
    pair[...] = stacked([mine[...], other[...]])


def tie(*arrays):
    count = len(arrays)
    return call(
        tie_kernel,
        "arrived",
        [jax.ShapeDtypeStruct(array.shape, array.dtype) for array in arrays],
        *arrays,
        places={i: pl.ANY for i in range(count)},
        aliases={i: i for i in range(count)},
    )


def grow_kernel(spans, mine, other, _, __, out, *___):
    a = mine[...].astype(F32)
    b = other[...].astype(F32)
    parts = [a[:spans], b[:spans], a[spans:] + b[spans:]]
    width = out.shape[1]
    pieces = [p[:, at : at + width] for at in range(0, a.shape[1], width) for p in parts]
    out[...] = jnp.concatenate(pieces, axis=0).astype(BF16)


def unfolded(state, width):
    state = state[...].astype(F32)
    count = state.shape[0] * state.shape[1] // width
    return jnp.concatenate(
        [state[at : at + count] for at in range(0, state.shape[0], count)], axis=1
    )


def split_stats(stats):
    lane = lax.broadcasted_iota(jnp.int32, stats.shape, 1)
    stats = jnp.where(lane < 16, stats, 0.0)
    high = stats.astype(BF16).astype(F32)
    rest = stats - high
    middle = rest.astype(BF16).astype(F32)
    low = (rest - middle).astype(BF16).astype(F32)
    packed = high + pltpu.roll(middle, 16, 1) + pltpu.roll(low, 32, 1)
    return packed.astype(BF16)


def joined_stats(packed):
    packed = packed.astype(F32)
    return packed + pltpu.roll(packed, 112, 1) + pltpu.roll(packed, 96, 1)


def queries_kernel(perm, mine, other, out):
    given = stacked([unfolded(state, out.shape[1]) for state in (mine, other)])
    out[...] = jnp.dot(perm[...], given, preferred_element_type=F32).astype(BF16)


def attention_kernel(
    heads, first_row, extras,
    picked, allowed, k0, k1, k2, k3, v0, v1, v2, v3, extra, *outs,
):
    rows = picked.shape[0] // 2
    half = slice(first_row, first_row + rows)
    message = len(outs) == 1
    queries = picked[half, :]
    wide = heads * GROUP * HD
    scaling = HD ** (-0.5)
    cached = k0.shape[0]
    stack = GROUP if rows * GROUP <= 128 else 1
    permit = jnp.concatenate([allowed[half, :]] * stack, axis=0) > 0.0
    nt = (((1,), (1,)), ((), ()))
    lane = iota((rows, HD), 1)
    stats = jnp.zeros((rows, HD), F32)

    def blocks_of(refs, g, first):
        columns = slice(g * HD, (g + 1) * HD)
        parts = [ref[0:cached, columns] for ref in refs]
        rest = [extra[first : first + extras, columns]]
        at = cached + first
        rest += [ref[at : at + extras, columns] for ref in (v1, v2, v3)]
        parts.append(jnp.concatenate(rest, axis=0))
        return parts

    def scores_of(head):
        q = jnp.concatenate(
            [queries[:, (head + i) * HD : (head + i + 1) * HD] for i in range(stack)], axis=0
        )
        scores = [
            lax.dot_general(q, key, nt, preferred_element_type=F32) * scaling
            for key in blocks_of((k0, k1, k2, k3), head // GROUP, 0)
        ]
        scores[-1] = jnp.where(permit, scores[-1], NEG)
        return scores

    def weights_of(scores):
        top = functools.reduce(jnp.maximum, scores[:-1]).max(axis=1, keepdims=True)
        top = jnp.maximum(top, scores[-1].max(axis=1, keepdims=True))
        weights = [jnp.exp(s - top) for s in scores]
        total = functools.reduce(jnp.add, weights[:-1]).sum(axis=1, keepdims=True)
        return top, total + weights[-1].sum(axis=1, keepdims=True), weights

    steps = range(0, heads * GROUP, stack)
    for first in range(0, len(steps), 4):
        group = steps[first : first + 4]
        scored = [scores_of(head) for head in group]
        weighed = [weights_of(scores) for scores in scored]
        for head, (top, total, weights) in zip(group, weighed):
            values = blocks_of((v0, v1, v2, v3), head // GROUP, extras)
            weights = [w.astype(BF16) for w in weights]
            out = jnp.dot(
                jnp.concatenate(weights[:-1], axis=1),
                jnp.concatenate(values[:-1], axis=0),
                preferred_element_type=F32,
            ) + jnp.dot(weights[-1], values[-1], preferred_element_type=F32)
            out = out / total
            level = top + jnp.log(total)
            for i in range(stack):
                at = i * rows
                columns = slice((head + i) * HD, (head + i + 1) * HD)
                outs[0][:, columns] = out[at : at + rows].astype(outs[0].dtype)
                stats = jnp.where(lane == head + i, level[at : at + rows], stats)
    if message:
        outs[0][:, wide:] = split_stats(stats)
    else:
        outs[1][...] = stats


def merge(heads, kept, kept_stats, got, first, rows):
    wide = heads * GROUP * HD
    half = slice(first, first + rows)
    mine = kept_stats[half, :]
    theirs = joined_stats(got[half, wide:])
    top = jnp.maximum(mine, theirs)
    a = jnp.exp(mine - top)
    b = jnp.exp(theirs - top)
    total = a + b
    a = a / total
    merged = []
    for h in range(heads * GROUP):
        columns = slice(h * HD, (h + 1) * HD)
        theirs = got[half, columns].astype(F32)
        merged.append(theirs + (kept[half, columns] - theirs) * a[:, h : h + 1])
    return merged, top + jnp.log(total)


def merge_kernel(heads, first, kept, kept_stats, got, *outs):
    wide = heads * GROUP * HD
    merged, stats = merge(heads, kept, kept_stats, got, first, kept.shape[0] // 2)
    for h, value in enumerate(merged):
        outs[0][:, h * HD : (h + 1) * HD] = value.astype(outs[0].dtype)
    if len(outs) == 1:
        outs[0][:, wide:] = split_stats(stats)
    else:
        outs[1][...] = stats


def last_kernel(heads, kept, kept_stats, got, out, squares):
    merged, _ = merge(heads, kept, kept_stats, got, 0, kept.shape[0])
    total = jnp.zeros_like(merged[0])
    for h, value in enumerate(merged):
        out[:, h * HD : (h + 1) * HD] = value
        total = total + value * value
    squares[...] = jnp.broadcast_to(total.sum(axis=1, keepdims=True), squares.shape)


def out_kernel(counts, columns_all, att, squares, other, gain, *outs):
    mean_sq = (squares[...] + other[...])[:, 0:1] / columns_all
    normed = att[...] * lax.rsqrt(mean_sq + EPS) * gain[...]
    at = 0
    for count, out in zip(counts, outs):
        out[...] = normed[at : at + count].astype(BF16)
        at += count


def per_device(
    cache_k,
    cache_v,
    span_q,
    span_k,
    span_v,
    span_frames,
    action_ids,
    action_table,
    frame_q,
    frame_k,
    frame_v,
    revealed_k,
    revealed_v,
    mask_k,
    mask_v,
    pass1_idx,
    pass2_idx,
    out_gain,
):
    owners = lax.axis_size("ctx")
    tp = lax.axis_size("tp")
    me = lax.axis_index("ctx")
    blocks = owners // 4
    spans = span_k.shape[0]
    frames = frame_k.shape[0]
    width = span_k.shape[1]
    q_width = span_q.shape[1]
    heads = width // HD
    n1 = pass1_idx.shape[0] // owners
    n2 = pass2_idx.shape[0] // owners
    picked = n1 + n2
    block_rows = -(-(spans + picked) // 8) * 8
    rows = blocks * block_rows

    bits = [(1 << b) + 1 for b in range(2, owners.bit_length() - 1)][::-1]

    depth = (blocks // 2) * spans + blocks * picked
    extras = -(-3 * spans // 16) * 16

    q3 = exchange(frame_q, "ctx", 3)
    small = (
        action_ids[None, :], pass1_idx[None, :], pass2_idx[None, :],
        action_table, span_k, span_v, frame_k, frame_v, revealed_k, revealed_v,
        mask_k, mask_v,
    )
    place = me.reshape(1)
    values, extra, token = call(
        functools.partial(keys_kernel, (spans, frames)),
        "plane_values",
        [
            jax.ShapeDtypeStruct((cache_v.shape[0] + 2 * extras, width), BF16),
            jax.ShapeDtypeStruct((2 * extras, width), BF16),
            jax.ShapeDtypeStruct((8, HD), F32),
        ],
        place, *small, cache_v,
        places={0: pltpu.SMEM, **{i + 1: pl.ANY for i in range(len(small) + 1)}},
        scratch=[pltpu.VMEM(array.shape, array.dtype) for array in small]
        + [pltpu.SemaphoreType.DMA((len(small) + 1,))],
        limit=PLAN_LIMIT,
        cost=pl.CostEstimate(flops=PLAN_FLOPS, bytes_accessed=PLAN_BYTES, transcendentals=0),
    )
    k0, chip, own_spans = call(
        stage_kernel,
        "queries_arrived",
        [
            jax.ShapeDtypeStruct(cache_k.shape, BF16),
            jax.ShapeDtypeStruct((2 * frames, q_width), BF16),
            jax.ShapeDtypeStruct(span_q.shape, BF16),
        ],
        cache_k, span_q, frame_q, q3,
    )
    other_chip = exchange(chip, "ctx", 1)
    idx1, idx2 = call(
        listed_kernel,
        "listed",
        [jax.ShapeDtypeStruct((1, idx.shape[0]), idx.dtype) for idx in (pass1_idx, pass2_idx)],
        token, pass1_idx[None, :], pass2_idx[None, :],
        places={0: pl.ANY},
        cost=pl.CostEstimate(flops=PLAN_FLOPS, bytes_accessed=PLAN_BYTES, transcendentals=0),
    )
    k3 = exchange(cache_k, "ctx", 3)
    v3 = exchange(values, "ctx", 3)
    k1 = exchange(k0, "ctx", 1)
    v1 = exchange(values, "ctx", 1)

    state = call(
        functools.partial(select_kernel, (spans, frames, n1, n2, len(bits))),
        "column_queries",
        jax.ShapeDtypeStruct((spans + blocks * picked, q_width), BF16),
        place, idx1, idx2, own_spans, chip, other_chip,
        places={0: pltpu.SMEM},
    )

    held = spans
    for bit in bits[:-1]:
        fold = 2 if bit == bits[-2] and (state.shape[0] + held) % 8 else 1
        other = exchange(state, "ctx", bit)
        state, k3, k1 = call(
            functools.partial(grow_kernel, held),
            "more_queries",
            [
                jax.ShapeDtypeStruct(
                    (fold * (state.shape[0] + held), q_width // fold), BF16
                ),
                jax.ShapeDtypeStruct(k3.shape, BF16),
                jax.ShapeDtypeStruct(k1.shape, BF16),
            ],
            state, other, k3, k1,
            places={2: pl.ANY, 3: pl.ANY},
            aliases={2: 1, 3: 2},
        )
        held = 2 * held
    other = exchange(state, "ctx", bits[-1])
    k2 = exchange(k3, "ctx", 1)
    other, v3, k2 = tie(other, v3, k2)
    v2 = exchange(v3, "ctx", 1)

    perm, allowed = call(
        functools.partial(plan_kernel, (spans, n1, n2, blocks, block_rows, len(bits), extras)),
        "row_plan",
        [
            jax.ShapeDtypeStruct((rows, 2 * depth), BF16),
            jax.ShapeDtypeStruct((rows, 4 * extras), F32),
        ],
        place, span_frames[None, :],
        places={0: pltpu.SMEM},
    )
    keep = rows // 2
    packed = q_width + HD
    queries = call(
        queries_kernel,
        "ordered_queries",
        jax.ShapeDtypeStruct((rows, q_width), BF16),
        perm, state, other,
    )
    given = (queries, allowed, k0, k1, k2, k3, cache_v, v1, v2, v3, extra)
    limit = (16 if blocks <= 4 else 40) * 2**20
    send = call(
        functools.partial(attention_kernel, heads, keep, extras),
        "sent_attention",
        jax.ShapeDtypeStruct((keep, packed), BF16),
        *given,
        limit=limit,
    )
    kept, stats = call(
        functools.partial(attention_kernel, heads, 0, extras),
        "kept_attention",
        [
            jax.ShapeDtypeStruct((keep, q_width), F32),
            jax.ShapeDtypeStruct((keep, HD), F32),
        ],
        *given,
        limit=limit,
    )
    for bit in bits[:0:-1]:
        got = exchange(send, "ctx", bit)
        keep = keep // 2
        given = (kept, stats, got)
        send = call(
            functools.partial(merge_kernel, heads, keep),
            "sent_partials",
            jax.ShapeDtypeStruct((keep, packed), BF16),
            *given,
        )
        kept, stats = call(
            functools.partial(merge_kernel, heads, 0),
            "kept_partials",
            [
                jax.ShapeDtypeStruct((keep, q_width), F32),
                jax.ShapeDtypeStruct((keep, HD), F32),
            ],
            *given,
        )
    got = exchange(send, "ctx", bits[0])
    att, squares = call(
        functools.partial(last_kernel, heads),
        "merge_last",
        [
            jax.ShapeDtypeStruct((block_rows, q_width), F32),
            jax.ShapeDtypeStruct((block_rows, HD), F32),
        ],
        kept, stats, got,
    )
    other_squares = exchange(squares, "tp", 1)
    counts = (spans, n1, n2)
    return tuple(
        call(
            functools.partial(out_kernel, counts, float(tp * q_width)),
            "normalize",
            [jax.ShapeDtypeStruct((count, q_width), BF16) for count in counts],
            att, squares, other_squares, out_gain[None, :],
        )
    )


def solution(mesh):
    in_specs = (
        P("ctx", "tp"),
        P("ctx", "tp"),
        P("ctx", "tp"),
        P("ctx", "tp"),
        P("ctx", "tp"),
        P(),
        P("ctx"),
        P(None, "tp"),
        P("ctx", "tp"),
        P("ctx", "tp"),
        P("ctx", "tp"),
        P("ctx", "tp"),
        P("ctx", "tp"),
        P("tp"),
        P("tp"),
        P(),
        P(),
        P("tp"),
    )
    out_specs = (P("ctx", "tp"), P("ctx", "tp"), P("ctx", "tp"))
    return jax.shard_map(
        per_device, mesh=mesh, in_specs=in_specs, out_specs=out_specs, check_vma=False
    )
```
